128 devices in a mesh: dp: 8 (over y, x_lo), seq: 8 (over z, core), pair: 2 (over x_hi).
Axes of the slice: x: 4 (x_hi: 2, x_lo: 2; x = x_hi * 2 + x_lo), y: 4, z: 4, core: 2. Of those that a mesh axis runs over, the one named last changes fastest.
Arguments:
- teacher_hidden: bfloat16 [2, 8, 2048, 5120], P('pair', 'dp', 'seq'), may hold values from -6 to 6
- student_query: bfloat16 [8, 2048, 5120], P('dp', ('seq', 'pair')), may hold values from -20 to 20
- student_key: bfloat16 [8, 2048, 5120], P('dp', ('seq', 'pair')), may hold values from -20 to 20
- student_value: bfloat16 [8, 2048, 5120], P('dp', ('seq', 'pair')), may hold values from -6 to 6
- residual: bfloat16 [8, 2048, 5120], P('dp', ('seq', 'pair')), may hold values from -6 to 6
- segment_ids: int32 [8, 2048], P('dp'), may hold values from 0 to 7, never falling along the last dimension, each value on 1 to 512 neighbouring positions
- timesteps: int32 [8, 8], P('dp'), may hold values from 0 to 999
- guide_scales: int32 [8, 8], P('dp'), may hold values from 8 to 64
- time_proj: bfloat16 [256, 10240], P(None, ('seq', 'pair')), may hold values from -0.375 to 0.375
- guide_proj: bfloat16 [256, 10240], P(None, ('seq', 'pair')), may hold values from -0.375 to 0.375
- teach_head: bfloat16 [5120, 64], replicated, may hold values from -0.078125 to 0.078125
- stud_head: bfloat16 [5120, 64], replicated, may hold values from -0.078125 to 0.078125
- out_proj: bfloat16 [5120, 5120], P('seq'), may hold values from -0.078125 to 0.078125
Outputs:
- grad_out_proj: float32 [5120, 5120], P('seq', ('dp', 'pair'))
- grad_head: float32 [5120, 64], P(('dp', 'seq', 'pair'))
- grad_guidance: float32 [256, 10240], P('dp', ('seq', 'pair'))
The draws below stay inside these ranges and needn't reach their ends.
All inputs are finite; a program needn't handle non-finite values.
Results may differ from the reference program's by a relative error of at most 0.027.
Values may be sent and summed in bfloat16 or wider, within the bound.
No kernel may reach another device: no remote copies, remote signals or barrier semaphores. Data moves between devices by JAX's collectives and lax.ppermute only.
A program may use at most 128 MiB of HBM per device.

```python
import math
import jax
import jax.numpy as jnp
import numpy as np
from jax import lax

D = 5120
HEADS = 40
HEAD_DIM = 128
FREQ = 256
PATCH = 64
SAMPLES = 8
PACK_LEN = 2048
PACKS = 8
TOKENS = 16384
MOST_LEN = 512
N_SEQ = 8


def draw_student_query(key, part):
    key = jax.random.fold_in(key, 11)
    drawn = jax.random.normal(key, (PACKS, PACK_LEN, D), jnp.float32)
    return (1.4 * jnp.clip(drawn, -6.0, 6.0)).astype(jnp.bfloat16)


def draw_student_key(key, part):
    key = jax.random.fold_in(key, 12)
    drawn = jax.random.normal(key, (PACKS, PACK_LEN, D), jnp.float32)
    return (1.4 * jnp.clip(drawn, -6.0, 6.0)).astype(jnp.bfloat16)


def set_ends(values, rng, least, high):
    longest = values.shape.index(max(values.shape))
    spots = []
    for shift in (0, 1):
        where = [jax.random.randint(jax.random.fold_in(rng, axis), (), 0, length) for axis, length in enumerate(values.shape)]
        where[longest] = (where[longest] + shift) % values.shape[longest]
        spots.append(tuple(where))
    return values.at[spots[0]].set(least).at[spots[1]].set(high)


def level_of(rng, dims, split, smallest, top_value):
    def one(dim, parts):
        draws = jax.random.uniform(jax.random.fold_in(jax.random.fold_in(rng, 6), dim), (parts,), jnp.float32, smallest / len(split), top_value / len(split))
        return jnp.repeat(jnp.exp(draws), dims[dim] // parts).reshape((-1,) + (1,) * (len(dims) - dim - 1))

    factor_of = one(*split[0])
    for cut in split[1:]:
        factor_of = factor_of * one(*cut)
    return factor_of


def profile(count, total, bound, skew):
    portions = [(1 << 20) // math.isqrt(rank ** skew) + 1 for rank in range(2, count + 1)]
    spare, counts = total - bound - (count - 1), [1] * (count - 1)
    while spare > 0:
        movable = [i for i in range(count - 1) if counts[i] < bound]
        whole, remaining = sum([portions[i] for i in movable]), spare
        for i in movable:
            addition = min(bound - counts[i], max(1, remaining * portions[i] // whole), spare)
            counts[i] = counts[i] + addition
            spare = spare - addition
    return np.array([bound] + counts)


def uneven(own_key, number_of, total, bound, slope):
    if number_of == 2:
        one = jax.random.randint(own_key, (), max(1, total - bound), min(bound, total - 1) + 1)
        return jnp.stack([one, total - one])
    sizes = jnp.asarray(profile(number_of, total, bound, slope), jnp.int32)
    pairs = (number_of - 1) // 2
    source_of, taker = sizes[1:1 + 2 * pairs:2], sizes[2:2 + 2 * pairs:2]
    room = jnp.minimum(source_of - 1, bound - taker)
    passed = jax.random.randint(jax.random.fold_in(own_key, 1), (pairs,), 0, 1 << 20) % (room + 1)
    sizes = sizes.at[1:1 + 2 * pairs:2].set(source_of - passed).at[2:2 + 2 * pairs:2].set(taker + passed)
    return sizes[jax.random.permutation(jax.random.fold_in(own_key, 2), number_of)]


def bell_draw(own_key, shape, deviation, most, cuts=(), kind=jnp.bfloat16):
    values = deviation * jax.random.normal(own_key, shape, jnp.float32)
    if cuts:
        values = values * level_of(own_key, shape, cuts, -0.22, 0.18)
    return jnp.clip(values, -most, most).astype(kind)


def setup_inputs(seed: int = 0) -> dict:
    arg_keys = jax.random.split(jax.random.key(seed), 14)
    return {
        "teacher_hidden": bell_draw(arg_keys[0], (2, PACKS, PACK_LEN, D), 1.0, 6.0, ((0, 2), (1, 8), (2, 8))),
        "student_query": draw_student_query(jax.random.fold_in(arg_keys[13], 71), 0),
        "student_key": draw_student_key(jax.random.fold_in(arg_keys[13], 71), 0),
        "student_value": bell_draw(arg_keys[3], (PACKS, PACK_LEN, D), 1.0, 6.0, ((0, 8), (1, 16))),
        "residual": bell_draw(arg_keys[4], (PACKS, PACK_LEN, D), 1.0, 6.0, ((0, 8), (1, 16))),
        "segment_ids": jax.vmap(lambda own: jnp.searchsorted(jnp.cumsum(uneven(own, SAMPLES, PACK_LEN, MOST_LEN, 2)), jnp.arange(PACK_LEN), side="right"))(jax.random.split(arg_keys[5], PACKS)).reshape((PACKS, PACK_LEN)).astype(jnp.int32),
        "timesteps": set_ends(jax.random.randint(arg_keys[6], (PACKS, SAMPLES), 0, 1000), jax.random.fold_in(arg_keys[6], 1), 0, 999).astype(jnp.int32),
        "guide_scales": set_ends(jax.random.randint(arg_keys[7], (PACKS, SAMPLES), 8, 65), jax.random.fold_in(arg_keys[7], 1), 8, 64).astype(jnp.int32),
        "time_proj": bell_draw(arg_keys[8], (FREQ, 2 * D), FREQ ** -0.5, 0.375, ((1, 16),)),
        "guide_proj": bell_draw(arg_keys[9], (FREQ, 2 * D), FREQ ** -0.5, 0.375, ((1, 16),)),
        "teach_head": bell_draw(arg_keys[10], (D, PATCH), D ** -0.5, 0.078125),
        "stud_head": bell_draw(arg_keys[11], (D, PATCH), D ** -0.5, 0.078125),
        "out_proj": bell_draw(arg_keys[12], (D, D), D ** -0.5, 0.078125, ((0, 8),)),
    }


def sinusoid(values, width):
    half = width // 2
    steps = jnp.arange(half, dtype=jnp.float32)
    freqs = jnp.exp(-math.log(10000.0) * steps / half)
    angles = values[..., None] * freqs
    return jnp.concatenate([jnp.cos(angles), jnp.sin(angles)], axis=-1)

def layer_norm(values):
    center = values - lax.optimization_barrier(jnp.mean(values, axis=-1, keepdims=True))
    inverse = lax.rsqrt(lax.optimization_barrier(jnp.mean(center * center, axis=-1, keepdims=True)) + 1e-06)
    return (center * inverse, inverse)

def pack_terms(time_proj, guide_proj, teach_head, stud_head, out_proj, hidden_pair, query, keyset, valueset, stream_in, segment, time_emb, guide_emb, guide_val):
    teach_mod = jnp.dot(time_emb, time_proj, preferred_element_type=jnp.float32)
    stud_mod = teach_mod + jnp.dot(guide_emb, guide_proj, preferred_element_type=jnp.float32)
    teach_tok = jnp.take(teach_mod, segment, axis=0)

    def teacher_out(hidden):
        normed_t = layer_norm(hidden.astype(jnp.float32))[0]
        model_in = (normed_t * (1.0 + teach_tok[:, D:]) + teach_tok[:, :D]).astype(jnp.bfloat16)
        return jnp.dot(model_in, teach_head, preferred_element_type=jnp.float32)
    cond_vel = teacher_out(hidden_pair[0])
    uncond_vel = teacher_out(hidden_pair[1])
    guide_tok = jnp.take(guide_val, segment, axis=0)[:, None]
    guided = uncond_vel + guide_tok * (cond_vel - uncond_vel)
    same = segment[:, None] == segment[None, :]

    def one_head(operands):
        head_q, head_k, head_v = operands
        scores = jnp.dot(head_q, head_k.T, preferred_element_type=jnp.float32) * (1.0 / math.sqrt(HEAD_DIM))
        scores = jnp.where(same, scores, -1e+30)
        top = lax.optimization_barrier(jnp.max(scores, axis=-1, keepdims=True))
        expo = jnp.exp(scores - top)
        probs = (expo / lax.optimization_barrier(jnp.sum(expo, axis=-1, keepdims=True))).astype(jnp.bfloat16)
        return jnp.dot(probs, head_v, preferred_element_type=jnp.float32).astype(jnp.bfloat16)

    def by_head(array):
        return array.reshape(PACK_LEN, HEADS, HEAD_DIM).transpose(1, 0, 2)
    heads_out = lax.map(one_head, (by_head(query), by_head(keyset), by_head(valueset)))
    attn_out = heads_out.transpose(1, 0, 2).reshape(PACK_LEN, D)
    group_width = D // N_SEQ
    groups_a = attn_out.reshape(PACK_LEN, N_SEQ, group_width).transpose(1, 0, 2)
    groups_w = out_proj.reshape(N_SEQ, group_width, D)

    def add_group(total, operands):
        part = jnp.dot(operands[0], operands[1], preferred_element_type=jnp.float32).astype(jnp.bfloat16)
        part = lax.optimization_barrier(part)
        return (total + part.astype(jnp.float32), None)
    attn_proj, _ = lax.scan(add_group, jnp.zeros((PACK_LEN, D), jnp.float32), (groups_a, groups_w))
    stream = stream_in.astype(jnp.float32) + attn_proj
    normed, inverse = layer_norm(stream)
    stud_tok = jnp.take(stud_mod, segment, axis=0)
    scale_tok = stud_tok[:, D:]
    stud_in = (normed * (1.0 + scale_tok) + stud_tok[:, :D]).astype(jnp.bfloat16)
    stud_vel = jnp.dot(stud_in, stud_head, preferred_element_type=jnp.float32)
    resid = ((stud_vel - guided) / math.sqrt(TOKENS)).astype(jnp.bfloat16)
    head_part = jnp.dot(stud_in.T, resid, preferred_element_type=jnp.float32)
    d_stud = jnp.dot(resid, stud_head.T, preferred_element_type=jnp.float32)
    onehot = (segment[:, None] == jnp.arange(SAMPLES, dtype=jnp.int32)[None, :]).astype(jnp.float32)
    d_mod = jnp.dot(onehot.T, jnp.concatenate([d_stud, d_stud * normed], axis=1), precision=lax.Precision.HIGHEST)
    guide_part = jnp.dot(guide_emb.astype(jnp.float32).T, d_mod, precision=lax.Precision.HIGHEST)
    dnorm = d_stud * (1.0 + scale_tok)
    d_proj = inverse * (dnorm - lax.optimization_barrier(jnp.mean(dnorm, axis=-1, keepdims=True)) - normed * lax.optimization_barrier(jnp.mean(dnorm * normed, axis=-1, keepdims=True)))
    d_proj = d_proj.astype(jnp.bfloat16)
    proj_part = jnp.dot(attn_out.T, d_proj, preferred_element_type=jnp.float32)
    return (proj_part, head_part, guide_part)

def reference(teacher_hidden, student_query, student_key, student_value, residual, segment_ids, timesteps, guide_scales, time_proj, guide_proj, teach_head, stud_head, out_proj):
    guidance = guide_scales.astype(jnp.float32) / 8.0
    t_emb = sinusoid(timesteps.astype(jnp.float32), FREQ).astype(jnp.bfloat16)
    g_emb = sinusoid(1000.0 * guidance, FREQ).astype(jnp.bfloat16)

    def step(carry, operands):
        terms = pack_terms(time_proj, guide_proj, teach_head, stud_head, out_proj, *operands)
        return ((carry[0] + terms[0], carry[1] + terms[1], carry[2] + terms[2]), None)
    start = (jnp.zeros((D, D), jnp.float32), jnp.zeros((D, PATCH), jnp.float32), jnp.zeros((FREQ, 2 * D), jnp.float32))
    operands = (teacher_hidden.transpose(1, 0, 2, 3), student_query, student_key, student_value, residual, segment_ids, t_emb, g_emb, guidance)
    totals, _ = lax.scan(step, start, operands)
    return (totals[0], totals[1], totals[2])
```

```python
import functools
import math

import jax
import jax.numpy as jnp
from jax import lax
from jax.experimental import pallas as pl
from jax.experimental.pallas import tpu as pltpu
from jax.sharding import PartitionSpec as P

HEAD_DIM = 128
VMEM_LIMIT = 56 * 1024 * 1024


def seq_shift(value, apart):
    pairs = [(i, ((i // 2 + apart) % 4) * 2 + i % 2) for i in range(8)]
    return lax.ppermute(value, "seq", pairs)


def core_swap(value):
    return lax.ppermute(value, "seq", [(i, i ^ 1) for i in range(8)])


def y_shift(value, apart):
    pairs = [(i, ((i // 2 + apart) % 4) * 2 + i % 2) for i in range(8)]
    return lax.ppermute(value, "dp", pairs)


def x_shift(value, apart):
    def target(index):
        y, x = index // 4, (index % 2) * 2 + (index // 2) % 2
        x = (x + apart) % 4
        return (y * 2 + x % 2) * 2 + x // 2

    return lax.ppermute(value, ("dp", "pair"), [(i, target(i)) for i in range(16)])


def pair_swap(value):
    return lax.ppermute(value, "pair", [(0, 1), (1, 0)])


def add_rows(left, right):
    return (left.astype(jnp.float32) + right.astype(jnp.float32)).astype(jnp.bfloat16)


def ring_reduce(block_at, shift, far=None):
    far = block_at(2) if far is None else far
    half = far.shape[0] // 2
    from_before = shift(far[:half], 1)
    from_after = shift(far[half:], 3)
    ahead, behind = block_at(1), block_at(3)
    ahead_alone = shift(ahead[half:], 1)
    behind_alone = shift(behind[:half], 3)
    ahead_sum = shift(add_rows(ahead[:half], from_before), 1)
    behind_sum = shift(add_rows(behind[half:], from_after), 3)
    return block_at(0), (ahead_sum, behind_alone), (ahead_alone, behind_sum)


def ring_gather(block):
    half = block.shape[0] // 2
    before = seq_shift(block, 1)
    after = seq_shift(block, 3)
    far_low = seq_shift(before[:half], 1)
    far_high = seq_shift(after[half:], 3)
    return [
        ([block], [core_swap(block)]),
        ([after], [core_swap(after)]),
        ([far_low, far_high], [core_swap(far_low), core_swap(far_high)]),
        ([before], [core_swap(before)]),
    ]


def sinusoid(values, width):
    half = width // 2
    steps = jnp.arange(half, dtype=jnp.float32)
    freqs = jnp.exp(-math.log(10000.0) * steps / half)
    angles = values[..., None] * freqs
    return jnp.concatenate([jnp.cos(angles), jnp.sin(angles)], axis=-1)


def dot_f32(left, right, left_dim, right_dim):
    return lax.dot_general(
        left, right, (((left_dim,), (right_dim,)), ((), ())), preferred_element_type=jnp.float32
    )


def teacher_kernel(hidden_ref, hot_ref, table_ref, head_ref, out_ref):
    rows, width = hidden_ref.shape
    chunks = table_ref.shape[0] // 2
    cols = width // chunks
    hidden = hidden_ref[...].astype(jnp.float32)
    center = hidden - jnp.mean(hidden, axis=-1, keepdims=True)
    inverse = lax.rsqrt(jnp.mean(center * center, axis=-1, keepdims=True) + 1e-06)
    hot = hot_ref[...]
    total = jnp.zeros((rows, head_ref.shape[1]), jnp.float32)
    for i in range(chunks):
        part = slice(i * cols, (i + 1) * cols)
        shift = dot_f32(hot, table_ref[i], 1, 0)
        scale = dot_f32(hot, table_ref[chunks + i], 1, 0)
        normed = center[:, part] * inverse
        model_in = (normed * (1.0 + scale) + shift).astype(jnp.bfloat16)
        total += dot_f32(model_in, head_ref[part, :], 1, 0)
    out_ref[...] = total


def teacher(hidden, hot, table, head):
    rows, width = hidden.shape
    block = 128
    patch = head.shape[1]
    return pl.pallas_call(
        teacher_kernel,
        grid=(rows // block,),
        in_specs=[
            pl.BlockSpec((block, width), lambda i: (i, 0)),
            pl.BlockSpec((block, hot.shape[1]), lambda i: (i, 0)),
            pl.BlockSpec(table.shape, lambda i: (0, 0, 0)),
            pl.BlockSpec(head.shape, lambda i: (0, 0)),
        ],
        out_specs=pl.BlockSpec((block, patch), lambda i: (i, 0)),
        out_shape=jax.ShapeDtypeStruct((rows, patch), jnp.float32),
        compiler_params=pltpu.CompilerParams(vmem_limit_bytes=VMEM_LIMIT),
        cost_estimate=pl.CostEstimate(
            flops=2 * rows * width * (patch + 32), bytes_accessed=6 * rows * width, transcendentals=rows
        ),
        name="teacher",
    )(hidden, hot, table, head)


def attend_kernel(
    low_ref, high_ref, place_ref, q_ref, qseg_ref, kseg_ref, ko_ref, kt_ref, vo_ref, vt_ref,
    out_ref, outt_ref, top_ref, sum_ref, acc_ref,
):
    heads = q_ref.shape[1] // HEAD_DIM
    step = pl.program_id(0)
    factor = math.log2(math.e) / math.sqrt(HEAD_DIM)
    top_ref[...] = jnp.full_like(top_ref, -1e30)
    sum_ref[...] = jnp.zeros_like(sum_ref)
    acc_ref[...] = jnp.zeros_like(acc_ref)
    query_seg = qseg_ref[0]

    def tile(index, carry):
        same = query_seg == kseg_ref[index]
        for h in range(heads):
            part = slice(h * HEAD_DIM, (h + 1) * HEAD_DIM)
            keys = jnp.concatenate([ko_ref[index, :, part], kt_ref[index, :, part]], axis=0)
            values = jnp.concatenate([vo_ref[index, :, part], vt_ref[index, :, part]], axis=0)
            scores = dot_f32(q_ref[:, part], keys, 1, 1) * factor
            scores = jnp.where(same, scores, -1e30)
            top_old = top_ref[h]
            top = jnp.maximum(top_old, jnp.max(scores, axis=-1, keepdims=True))
            expo = jnp.exp2(scores - top)
            keep = jnp.exp2(top_old - top)
            top_ref[h] = top
            sum_ref[h] = sum_ref[h] * keep + jnp.sum(expo, axis=-1, keepdims=True)
            acc_ref[h] = acc_ref[h] * keep + dot_f32(expo.astype(jnp.bfloat16), values, 1, 0)
        return carry

    lax.fori_loop(low_ref[step], high_ref[step], tile, 0)
    for h in range(heads):
        part = slice(h * HEAD_DIM, (h + 1) * HEAD_DIM)
        result = acc_ref[h] / sum_ref[h]
        out_ref[0, 0, :, part] = result.astype(jnp.bfloat16)
        outt_ref[0, part, :] = result.T.astype(jnp.bfloat16)


def attend(low, high, place, query, query_seg, key_seg, key_own, key_other, value_own, value_other):
    rows, width = query.shape
    blocks, block = query_seg.shape[0], query_seg.shape[1]
    heads = width // HEAD_DIM

    def chip(j, place_ref):
        return (j // 2 - place_ref[0] + 4) % 4

    def core(j, place_ref):
        return (j % 2 + place_ref[1]) % 2

    whole = pl.BlockSpec(key_own.shape, lambda j, lo, hi, p: (0, 0, 0))
    return pl.pallas_call(
        attend_kernel,
        grid_spec=pltpu.PrefetchScalarGridSpec(
            num_scalar_prefetch=3,
            grid=(blocks,),
            in_specs=[
                pl.BlockSpec((block, width), lambda j, lo, hi, p: (j, 0)),
                pl.BlockSpec((1, block, 1), lambda j, lo, hi, p: (j, 0, 0)),
                pl.BlockSpec(key_seg.shape, lambda j, lo, hi, p: (0, 0, 0)),
                whole, whole, whole, whole,
            ],
            out_specs=[
                pl.BlockSpec((1, 1, block, width), lambda j, lo, hi, p: (core(j, p), chip(j, p), 0, 0)),
                pl.BlockSpec((1, width, block), lambda j, lo, hi, p: (chip(j, p), 0, core(j, p))),
            ],
            scratch_shapes=[
                pltpu.VMEM((heads, block, 1), jnp.float32),
                pltpu.VMEM((heads, block, 1), jnp.float32),
                pltpu.VMEM((heads, block, HEAD_DIM), jnp.float32),
            ],
        ),
        out_shape=[
            jax.ShapeDtypeStruct((2, blocks // 2, block, width), jnp.bfloat16),
            jax.ShapeDtypeStruct((blocks // 2, width, 2 * block), jnp.bfloat16),
        ],
        compiler_params=pltpu.CompilerParams(vmem_limit_bytes=VMEM_LIMIT),
        cost_estimate=pl.CostEstimate(
            flops=4 * rows * 768 * width, bytes_accessed=14 * rows * width, transcendentals=rows * 768 * heads
        ),
        name="attend",
    )(low, high, place, query, query_seg, key_seg, key_own, key_other, value_own, value_other)


def student_kernel(
    own_ref, la_ref, lb_ref, ha_ref, hb_ref, residual_ref, hot_ref, table_ref, head_ref, guided_ref,
    dproj_ref, headpart_ref, mod_ref, stream_ref, normed_ref, in_ref, dn_ref,
):
    rows, width = residual_ref.shape
    half = rows // 2
    chunks = table_ref.shape[0] // 2
    cols = width // chunks
    f32 = jnp.float32
    total = jnp.zeros((rows, 1), f32)
    for i in range(chunks):
        part = slice(i * cols, (i + 1) * cols)
        low = la_ref[:, part].astype(f32) + lb_ref[:, part].astype(f32)
        high = ha_ref[:, part].astype(f32) + hb_ref[:, part].astype(f32)
        base = residual_ref[:, part].astype(f32) + own_ref[:, part].astype(f32)
        stream = base + jnp.concatenate([low, high], axis=0)
        stream_ref[:, part] = stream
        total += jnp.sum(stream, axis=-1, keepdims=True)
    mean = total / width
    square = jnp.zeros((rows, 1), f32)
    for i in range(chunks):
        part = slice(i * cols, (i + 1) * cols)
        center = stream_ref[:, part] - mean
        square += jnp.sum(center * center, axis=-1, keepdims=True)
    inverse = lax.rsqrt(square / width + 1e-06)
    hot = hot_ref[...]
    velocity = jnp.zeros((rows, head_ref.shape[1]), f32)
    for i in range(chunks):
        part = slice(i * cols, (i + 1) * cols)
        normed = (stream_ref[:, part] - mean) * inverse
        shift = dot_f32(hot, table_ref[i], 1, 0)
        scale = 1.0 + dot_f32(hot, table_ref[chunks + i], 1, 0)
        model_in = (normed * scale + shift).astype(jnp.bfloat16)
        normed_ref[:, part] = normed
        dn_ref[:, part] = scale
        in_ref[:, part] = model_in
        velocity += dot_f32(model_in, head_ref[part, :], 1, 0)
    scale_back = 1.0 / math.sqrt(16384)
    resid = ((velocity - guided_ref[...]) * scale_back).astype(jnp.bfloat16)
    first = jnp.zeros((rows, 1), f32)
    second = jnp.zeros((rows, 1), f32)
    samples = mod_ref.shape[1]
    hot_rows = hot[:, hot.shape[1] - samples :]
    for i in range(chunks):
        part = slice(i * cols, (i + 1) * cols)
        cotangent = dot_f32(resid, head_ref[part, :], 1, 1)
        headpart_ref[part, :] = dot_f32(in_ref[:, part], resid, 0, 0).astype(jnp.bfloat16)
        normed = normed_ref[:, part]
        mod_ref[i] = dot_f32(hot_rows, cotangent.astype(jnp.bfloat16), 0, 0).astype(jnp.bfloat16)
        mod_ref[chunks + i] = dot_f32(
            hot_rows, (cotangent * normed).astype(jnp.bfloat16), 0, 0
        ).astype(jnp.bfloat16)
        dnorm = cotangent * dn_ref[:, part]
        dn_ref[:, part] = dnorm
        first += jnp.sum(dnorm, axis=-1, keepdims=True)
        second += jnp.sum(dnorm * normed, axis=-1, keepdims=True)
    first = first / width
    second = second / width

    def back(chunk):
        part = slice(chunk * cols, (chunk + 1) * cols)
        return inverse * (dn_ref[:, part] - first - normed_ref[:, part] * second)

    side = cols // 2
    for lo in range(2):
        for y in range(0, 4, 2):
            even, odd = back(2 * y + lo), back(2 * y + 2 + lo)
            for hi in range(2):
                cut = slice(hi * side, (hi + 1) * side)
                both = jnp.concatenate([even[:, cut], odd[:, cut]], axis=1)
                dproj_ref[hi * 2 + lo, :, (y // 2) * cols : (y // 2 + 1) * cols] = both.astype(jnp.bfloat16)


def student(own, low, high, residual, hot, table, head, guided):
    rows, width = residual.shape
    samples = 8
    chunk = table.shape[2]
    return pl.pallas_call(
        student_kernel,
        out_shape=[
            jax.ShapeDtypeStruct((4, rows, width // 4), jnp.bfloat16),
            jax.ShapeDtypeStruct(head.shape, jnp.bfloat16),
            jax.ShapeDtypeStruct((table.shape[0], samples, chunk), jnp.bfloat16),
        ],
        scratch_shapes=[
            pltpu.VMEM((rows, width), jnp.float32),
            pltpu.VMEM((rows, width), jnp.float32),
            pltpu.VMEM((rows, width), jnp.bfloat16),
            pltpu.VMEM((rows, width), jnp.float32),
        ],
        compiler_params=pltpu.CompilerParams(vmem_limit_bytes=VMEM_LIMIT),
        cost_estimate=pl.CostEstimate(
            flops=2 * rows * width * 400, bytes_accessed=12 * rows * width, transcendentals=rows
        ),
        name="student",
    )(own, *low, *high, residual, hot, table, head, guided)


def grad_kernel(layout, sources, *refs):
    left_refs = refs[:sources]
    right_refs = refs[sources:-1]
    out_ref = refs[-1]
    total = jnp.zeros((left_refs[0].shape[1], out_ref.shape[0]), jnp.float32)
    for source, chip, pieces in layout:
        rows = jnp.concatenate([right_refs[k][start : start + size, :] for k, start, size in pieces], axis=0)
        total += dot_f32(left_refs[source][chip], rows, 1, 0)
    out_ref[...] = total.T.astype(jnp.bfloat16)


def grad_product(lefts, groups):
    rights, layout = [], []
    for gathered, sources in groups:
        for chip, cores in enumerate(gathered):
            spans = [[], []]
            for core, pieces in enumerate(cores):
                for piece in pieces:
                    spans[core].append((len(rights), piece.shape[0]))
                    rights.append(piece)
            for position, source in enumerate(sources):
                parts = []
                for core in range(2):
                    begin, end = position * 128, (position + 1) * 128
                    offset = 0
                    for index, size in spans[core]:
                        lo, hi = max(begin, offset), min(end, offset + size)
                        if lo < hi:
                            parts.append((index, lo - offset, hi - lo))
                        offset += size
                layout.append((source, chip, parts))
    tile = 256
    depth, width = lefts[0].shape[1], rights[0].shape[1]
    return pl.pallas_call(
        functools.partial(grad_kernel, layout, len(lefts)),
        grid=(width // tile,),
        in_specs=[pl.BlockSpec(left.shape, lambda i: (0, 0, 0)) for left in lefts]
        + [pl.BlockSpec((right.shape[0], tile), lambda i: (0, i)) for right in rights],
        out_specs=pl.BlockSpec((tile, depth), lambda i: (i, 0)),
        out_shape=jax.ShapeDtypeStruct((width, depth), jnp.bfloat16),
        compiler_params=pltpu.CompilerParams(vmem_limit_bytes=VMEM_LIMIT),
        cost_estimate=pl.CostEstimate(
            flops=2 * 4096 * depth * width, bytes_accessed=2 * 4096 * (depth + width), transcendentals=0
        ),
        name="grad_product",
    )(*lefts, *rights)


def local(
    teacher_hidden,
    student_query,
    student_key,
    student_value,
    residual,
    segment_ids,
    timesteps,
    guide_scales,
    time_proj,
    guide_proj,
    teach_head,
    stud_head,
    out_proj,
):
    bf16, f32 = jnp.bfloat16, jnp.float32
    seq_pos, pair_pos, data_pos = lax.axis_index("seq"), lax.axis_index("pair"), lax.axis_index("dp")
    chip_z, core = seq_pos // 2, seq_pos % 2
    chip_y, chip_x = data_pos // 2, pair_pos * 2 + data_pos % 2
    segment = segment_ids[0]
    samples = timesteps.shape[1]
    freq = time_proj.shape[0]

    guidance = guide_scales[0].astype(f32) / 8.0
    t_emb = sinusoid(timesteps[0].astype(f32), freq).astype(bf16)
    g_emb = sinusoid(1000.0 * guidance, freq).astype(bf16)
    teach_cols = jnp.dot(t_emb, time_proj, preferred_element_type=f32)
    stud_cols = teach_cols + jnp.dot(g_emb, guide_proj, preferred_element_type=f32)
    columns = jnp.concatenate([teach_cols, stud_cols], axis=0).astype(bf16)
    table = lax.all_to_all(
        jnp.broadcast_to(columns[None], (16,) + columns.shape), ("seq", "pair"), 0, 0, tiled=True
    )
    all_guidance = lax.all_to_all(
        jnp.broadcast_to(guidance[None], (8, samples)), "dp", 0, 0, tiled=True
    ).reshape(-1)
    all_emb = sinusoid(1000.0 * all_guidance, freq).astype(bf16)
    emb_cols = lax.dynamic_slice_in_dim(all_emb, data_pos * (freq // 8), freq // 8, 1)

    hidden = teacher_hidden[0, 0]
    stud_rows = student_query.shape[1]
    ids = jnp.arange(2 * samples, dtype=jnp.int32)[None, :]
    teach_seg = lax.dynamic_slice_in_dim(segment, seq_pos * hidden.shape[0], hidden.shape[0])
    stud_seg = lax.dynamic_slice_in_dim(teach_seg, pair_pos * stud_rows, stud_rows)
    teach_hot = (teach_seg[:, None] == ids).astype(bf16)
    stud_hot = (stud_seg[:, None] == ids - samples).astype(bf16)
    velocity = teacher(hidden, teach_hot, table, teach_head)
    own_vel = lax.dynamic_slice_in_dim(velocity, pair_pos * stud_rows, stud_rows, 0)
    sent_vel = lax.dynamic_slice_in_dim(velocity, (1 - pair_pos) * stud_rows, stud_rows, 0)
    other_vel = pair_swap(sent_vel.astype(bf16)).astype(f32)
    cond_vel = jnp.where(pair_pos == 0, own_vel, other_vel)
    uncond_vel = jnp.where(pair_pos == 0, other_vel, own_vel)
    guide_tok = jnp.sum(
        jnp.where(stud_seg[:, None] == ids[:, :samples], guidance[None, :], 0.0), axis=1, keepdims=True
    )
    guided = uncond_vel + guide_tok * (cond_vel - uncond_vel)

    key_own = lax.all_to_all(student_key[0], "seq", split_axis=1, concat_axis=0, tiled=True)
    value_own = lax.all_to_all(student_value[0], "seq", split_axis=1, concat_axis=0, tiled=True)
    query = lax.all_to_all(student_query[0], "seq", split_axis=1, concat_axis=0, tiled=True)
    key_other, value_other = pair_swap(key_own), pair_swap(value_own)
    by_block = segment.reshape(8, 2, stud_rows)
    own_seg = lax.dynamic_index_in_dim(by_block, pair_pos, 1, keepdims=False)
    other_seg = lax.dynamic_index_in_dim(by_block, 1 - pair_pos, 1, keepdims=False)
    low = jnp.sum((segment[None, :] < own_seg[:, :1]).astype(jnp.int32), axis=1) // 256
    high = (jnp.sum((segment[None, :] <= own_seg[:, -1:]).astype(jnp.int32), axis=1) + 255) // 256
    place = jnp.stack([chip_z, core]).astype(jnp.int32)
    blocks = (8, stud_rows, query.shape[1])
    attn, attn_t = attend(
        low,
        high,
        place,
        query,
        own_seg[:, :, None],
        jnp.concatenate([own_seg, other_seg], axis=1)[:, None, :],
        key_own.reshape(blocks),
        key_other.reshape(blocks),
        value_own.reshape(blocks),
        value_other.reshape(blocks),
    )

    weights = jnp.concatenate([out_proj, core_swap(out_proj)], axis=0)
    attn_both = jnp.concatenate([attn[0], core_swap(attn[1])], axis=-1)
    far = jnp.dot(attn_both[2], weights, preferred_element_type=f32).astype(bf16)
    near = jnp.dot(
        jnp.concatenate([attn_both[1], attn_both[3], attn_both[0]], axis=0),
        weights,
        preferred_element_type=f32,
    ).astype(bf16)
    order = {1: 0, 3: 1, 0: 2}
    own, low_rows, high_rows = ring_reduce(
        lambda apart: near[order[apart] * stud_rows : (order[apart] + 1) * stud_rows], seq_shift, far
    )
    attn_ts = [attn_t] + [x_shift(attn_t, apart) for apart in (1, 3, 2)]

    d_proj, head_part, mod_part = student(
        own, low_rows, high_rows, residual[0], stud_hot, table, stud_head, guided
    )

    mine = lax.dynamic_index_in_dim(d_proj, chip_x, 0, keepdims=False)
    from_x = jnp.concatenate(
        [
            x_shift(lax.dynamic_index_in_dim(d_proj, (chip_x + apart) % 4, 0, keepdims=False), apart)
            for apart in (1, 3, 2)
        ],
        axis=0,
    )
    product = grad_product(attn_ts, [(ring_gather(mine), (0,)), (ring_gather(from_x), (1, 2, 3))])
    product = product.reshape(4, product.shape[0] // 4, product.shape[1])
    own_grad, low_grad, high_grad = ring_reduce(
        lambda apart: lax.dynamic_index_in_dim(product, (chip_y + apart) % 4, 0, keepdims=False), y_shift
    )
    rest = jnp.concatenate(
        [
            low_grad[0].astype(f32) + low_grad[1].astype(f32),
            high_grad[0].astype(f32) + high_grad[1].astype(f32),
        ],
        axis=0,
    )
    grad_out_proj = (own_grad.astype(f32) + rest).T

    mod_terms = lax.all_to_all(mod_part, ("seq", "pair"), 0, 0, tiled=True)
    d_mod = jnp.sum(mod_terms.astype(f32), axis=0).astype(bf16)
    d_mods = lax.all_to_all(
        jnp.broadcast_to(d_mod[None], (8,) + d_mod.shape), "dp", 0, 0, tiled=True
    ).reshape(8 * samples, -1)
    grad_guidance = dot_f32(emb_cols, d_mods, 0, 0)

    head_terms = lax.all_to_all(
        head_part.reshape(128, -1, head_part.shape[1]), ("dp", "seq", "pair"), 0, 0, tiled=True
    )
    grad_head = jnp.sum(head_terms.astype(f32), axis=0)
    return (grad_out_proj, grad_head, grad_guidance)


def solution(mesh):
    placed = (
        P("pair", "dp", "seq", None),
        P("dp", ("seq", "pair"), None),
        P("dp", ("seq", "pair"), None),
        P("dp", ("seq", "pair"), None),
        P("dp", ("seq", "pair"), None),
        P("dp", None),
        P("dp", None),
        P("dp", None),
        P(None, ("seq", "pair")),
        P(None, ("seq", "pair")),
        P(),
        P(),
        P("seq", None),
    )
    return jax.shard_map(
        local,
        mesh=mesh,
        in_specs=placed,
        out_specs=(
            P("seq", ("dp", "pair")),
            P(("dp", "seq", "pair"), None),
            P("dp", ("seq", "pair")),
        ),
        check_vma=False,
    )
```

```python
import functools
import math

import jax
import jax.numpy as jnp
from jax import lax
from jax.experimental import pallas as pl
from jax.experimental.pallas import tpu as pltpu
from jax.sharding import PartitionSpec as P

HEAD_DIM = 128
VMEM_LIMIT = 56 * 1024 * 1024
FREE = pl.CostEstimate(flops=0, bytes_accessed=0, transcendentals=0)


def side(core):
    return 1 if core == 0 else -1


def seq_shift(value, apart):
    return lax.ppermute(value, "seq", [(i, ((i // 2 + apart) % 4) * 2 + i % 2) for i in range(8)])


def seq_ring(value):
    return lax.ppermute(value, "seq", [(i, ((i // 2 + side(i % 2)) % 4) * 2 + i % 2) for i in range(8)])


def core_swap(value):
    return lax.ppermute(value, "seq", [(i, i ^ 1) for i in range(8)])


def y_shift(value, apart):
    return lax.ppermute(value, "dp", [(i, ((i // 2 + apart) % 4) * 2 + i % 2) for i in range(8)])


def x_shift(value, apart):
    def target(index):
        data, seq, pair = index // 16, index // 2 % 8, index % 2
        x = (pair * 2 + data % 2 + side(seq % 2) * apart) % 4
        return (data // 2 * 2 + x % 2) * 16 + seq * 2 + x // 2

    return lax.ppermute(value, ("dp", "seq", "pair"), [(i, target(i)) for i in range(128)])


def pair_swap(value):
    return lax.ppermute(value, "pair", [(0, 1), (1, 0)])


def add_rows(left, right):
    return (left.astype(jnp.float32) + right.astype(jnp.float32)).astype(jnp.bfloat16)


def ring_reduce(low, high):
    totals = [seq_ring(low[0]), seq_ring(high[0])]
    for terms in zip(low[1:], high[1:]):
        totals = [seq_ring(add_rows(term, total)) for term, total in zip(terms, totals)]
    return totals


def ring_gather(block):
    blocks = [block]
    for _ in range(3):
        blocks.append(seq_ring(blocks[-1]))
    return blocks


def sinusoid(values, width):
    half = width // 2
    steps = jnp.arange(half, dtype=jnp.float32)
    freqs = jnp.exp(-math.log(10000.0) * steps / half)
    angles = values[..., None] * freqs
    return jnp.concatenate([jnp.cos(angles), jnp.sin(angles)], axis=-1)


def dot_f32(left, right, left_dim, right_dim):
    return lax.dot_general(
        left, right, (((left_dim,), (right_dim,)), ((), ())), preferred_element_type=jnp.float32
    )


def teacher_kernel(hidden_ref, hot_ref, table_ref, head_ref, out_ref):
    rows, width = hidden_ref.shape
    chunks = table_ref.shape[0] // 2
    cols = width // chunks
    hidden = hidden_ref[...].astype(jnp.float32)
    center = hidden - jnp.mean(hidden, axis=-1, keepdims=True)
    inverse = lax.rsqrt(jnp.mean(center * center, axis=-1, keepdims=True) + 1e-06)
    hot = hot_ref[...]
    total = jnp.zeros((rows, head_ref.shape[0]), jnp.float32)
    for i in range(chunks):
        part = slice(i * cols, (i + 1) * cols)
        shift = dot_f32(hot, table_ref[i], 1, 0)
        scale = dot_f32(hot, table_ref[chunks + i], 1, 0)
        normed = center[:, part] * inverse
        model_in = (normed * (1.0 + scale) + shift).astype(jnp.bfloat16)
        total += dot_f32(model_in, head_ref[:, part], 1, 1)
    out_ref[...] = total


def teacher(hidden, hot, table, head):
    rows, width = hidden.shape
    block = 128
    patch = head.shape[0]
    return pl.pallas_call(
        teacher_kernel,
        grid=(rows // block,),
        in_specs=[
            pl.BlockSpec((block, width), lambda i: (i, 0)),
            pl.BlockSpec((block, hot.shape[1]), lambda i: (i, 0)),
            pl.BlockSpec(table.shape, lambda i: (0, 0, 0)),
            pl.BlockSpec(head.shape, lambda i: (0, 0)),
        ],
        out_specs=pl.BlockSpec((block, patch), lambda i: (i, 0)),
        out_shape=jax.ShapeDtypeStruct((rows, patch), jnp.float32),
        compiler_params=pltpu.CompilerParams(vmem_limit_bytes=VMEM_LIMIT),
        cost_estimate=FREE,
        name="teacher",
    )(hidden, hot, table, head)


def pack_kernel(tensors, *refs):
    out_ref = refs[-1]
    groups = out_ref.shape[0]
    for g in range(groups):
        start = 0
        for ref in [refs[t * groups + g] for t in range(tensors)] + list(refs[tensors * groups : -1]):
            out_ref[g, start : start + ref.shape[0]] = ref[...]
            start += ref.shape[0]


def exchange(tensors, *shared):
    rows, width = tensors[0].shape
    groups, count = 8, len(tensors)
    cols = width // groups
    half = groups // 2
    height = count * rows + sum(array.shape[0] for array in shared)
    packed = pl.pallas_call(
        functools.partial(pack_kernel, count),
        grid=(2,),
        in_specs=[
            pl.BlockSpec((rows, cols), functools.partial(lambda g, i: (0, i * half + g), g))
            for _ in tensors
            for g in range(half)
        ]
        + [pl.BlockSpec(array.shape, lambda i: (0, 0)) for array in shared],
        out_specs=pl.BlockSpec((half, height, cols), lambda i: (i, 0, 0)),
        out_shape=jax.ShapeDtypeStruct((groups, height, cols), tensors[0].dtype),
        compiler_params=pltpu.CompilerParams(vmem_limit_bytes=VMEM_LIMIT),
        cost_estimate=FREE,
        name="pack",
    )(*[tensor for tensor in tensors for _ in range(half)], *shared)
    return lax.all_to_all(packed, "seq", 0, 0, tiled=True)


def rows_kernel(in_ref, out_ref):
    out_ref[...] = in_ref[...]


def take_rows(pieces, start, rows):
    blocks, _, cols = pieces.shape
    half = blocks // 2
    return pl.pallas_call(
        rows_kernel,
        grid=(2,),
        in_specs=[pl.BlockSpec((half, rows, cols), lambda i: (i, start // rows, 0))],
        out_specs=pl.BlockSpec((half, rows, cols), lambda i: (i, 0, 0)),
        out_shape=jax.ShapeDtypeStruct((blocks, rows, cols), pieces.dtype),
        compiler_params=pltpu.CompilerParams(vmem_limit_bytes=VMEM_LIMIT),
        cost_estimate=FREE,
        name="take_rows",
    )(pieces)


def attend_kernel(
    low_ref, high_ref, turn_ref, qseg_ref, kseg_ref, value_ref, first_ref, second_ref,
    out_ref, cross_ref, turned_ref, score_ref, top_ref, acc_ref,
):
    block = value_ref.shape[1]
    heads = value_ref.shape[2] // HEAD_DIM
    upper, lower = slice(0, block), slice(block, 2 * block)
    step = pl.program_id(0)
    low, high = low_ref[step], high_ref[step]
    factor = math.log2(math.e) / math.sqrt(HEAD_DIM)
    parts = [slice(h * HEAD_DIM, (h + 1) * HEAD_DIM) for h in range(heads)]
    top_ref[...] = jnp.full_like(top_ref, -1e30)
    acc_ref[...] = jnp.zeros_like(acc_ref)
    query_seg = qseg_ref[0]

    def score(index, carry):
        same = query_seg == kseg_ref[index]
        scores = [
            dot_f32(first_ref[turn_ref[step], lower, part], second_ref[index, :, part], 1, 1) for part in parts
        ]
        for h in range(heads):
            masked = jnp.where(same, scores[h] * factor, -1e30)
            score_ref[index - low, h] = masked
            pair = jnp.maximum(masked[:, :block], masked[:, block:])
            top_ref[h] = jnp.maximum(top_ref[h], pair)
        return carry

    lax.fori_loop(low, high, score, 0)
    for h in range(heads):
        top_ref[h] = jnp.broadcast_to(jnp.max(top_ref[h], axis=-1, keepdims=True), top_ref.shape[1:])
    ones = jnp.ones((2 * block, HEAD_DIM), jnp.bfloat16)

    def mix(index, carry):
        weights = []
        for h in range(heads):
            top = jnp.concatenate([top_ref[h], top_ref[h]], axis=1)
            weights.append(jnp.exp2(score_ref[index - low, h] - top).astype(jnp.bfloat16))
        for h, part in enumerate(parts):
            values = jnp.concatenate([first_ref[index, upper, part], value_ref[index, :, part]], axis=0)
            acc_ref[h] += dot_f32(weights[h], jnp.concatenate([values, ones], axis=1), 1, 0)
        return carry

    lax.fori_loop(low, high, mix, 0)
    result = jnp.concatenate(
        [acc_ref[h, :, :HEAD_DIM] / acc_ref[h, :, HEAD_DIM:] for h in range(heads)], axis=1
    )
    rounded = result.astype(jnp.bfloat16)

    @pl.when(step < 4)
    def _():
        out_ref[0] = rounded

    @pl.when(step >= 4)
    def _():
        cross_ref[0] = rounded

    turned = result.T.astype(jnp.bfloat16)
    arrival = lax.rem(8 - step, 4)
    for core in range(2):

        @pl.when(step // 4 == core)
        def _():
            turned_ref[arrival, :, core * block : (core + 1) * block] = turned


def attend(low, high, turn, query_seg, key_seg, value_other, first, second):
    blocks, block, width = value_other.shape
    chips = blocks // 2
    heads = width // HEAD_DIM

    def fixed(array):
        return pl.BlockSpec(array.shape, lambda j, *_: (0,) * array.ndim, pipeline_mode=pl.Buffered(1))

    return pl.pallas_call(
        attend_kernel,
        grid_spec=pltpu.PrefetchScalarGridSpec(
            num_scalar_prefetch=3,
            grid=(blocks,),
            in_specs=[pl.BlockSpec((1, block, 1), lambda j, *_: (j, 0, 0))]
            + [fixed(array) for array in (key_seg, value_other, first, second)],
            out_specs=[
                pl.BlockSpec((1, block, width), lambda j, *_: (jnp.minimum(j, 3), 0, 0)),
                pl.BlockSpec((1, block, width), lambda j, *_: (jnp.maximum(j - 4, 0), 0, 0)),
                pl.BlockSpec((chips, width, 2 * block), lambda j, *_: (0, 0, 0)),
            ],
            scratch_shapes=[
                pltpu.VMEM((6, heads, block, 2 * block), jnp.float32),
                pltpu.VMEM((heads, block, block), jnp.float32),
                pltpu.VMEM((heads, block, 2 * HEAD_DIM), jnp.float32),
            ],
        ),
        out_shape=[
            jax.ShapeDtypeStruct((chips, block, width), jnp.bfloat16),
            jax.ShapeDtypeStruct((chips, block, width), jnp.bfloat16),
            jax.ShapeDtypeStruct((chips, width, 2 * block), jnp.bfloat16),
        ],
        compiler_params=pltpu.CompilerParams(vmem_limit_bytes=VMEM_LIMIT),
        cost_estimate=FREE,
        name="attend",
    )(low, high, turn, query_seg, key_seg, value_other, first, second)


def project_kernel(own_ref, crossed_ref, w_own_ref, w_crossed_ref, *refs):
    outs, left_ref = refs[:-1], refs[-1]
    chips, block, depth = own_ref.shape

    @pl.when(pl.program_id(0) == 0)
    def _():
        for k in range(chips):
            take, even = slice(k * block, (k + 1) * block), depth // 256 * 256
            left_ref[take, :even] = own_ref[k, :, :even]
            left_ref[take, even : 2 * even] = crossed_ref[k, :, :even]
            left_ref[take, 2 * even : depth + even] = own_ref[k, :, even:]
            left_ref[take, depth + even :] = crossed_ref[k, :, even:]

    even = depth // 256 * 256
    rest = jnp.concatenate([w_own_ref[even:, :], w_crossed_ref[even:, :]], axis=0)
    total = dot_f32(left_ref[:, :even], w_own_ref[:even, :], 1, 0)
    total += dot_f32(left_ref[:, even : 2 * even], w_crossed_ref[:even, :], 1, 0)
    total = (total + dot_f32(left_ref[:, 2 * even :], rest, 1, 0)).astype(jnp.bfloat16)
    start = 0
    for out in outs:
        out[...] = total[start : start + out.shape[0]]
        start += out.shape[0]


def project(own, crossed, w_own, w_crossed):
    chips, block, depth = own.shape
    width = w_own.shape[1]
    tile = 1024
    heights = [block] + [block // 2] * (2 * chips - 2)
    left = pl.BlockSpec(own.shape, lambda i: (0, 0, 0))
    right = pl.BlockSpec((depth, tile), lambda i: (0, i))
    return pl.pallas_call(
        project_kernel,
        grid=(width // tile,),
        in_specs=[left, left, right, right],
        out_specs=[pl.BlockSpec((height, tile), lambda i: (0, i)) for height in heights],
        out_shape=[jax.ShapeDtypeStruct((height, width), jnp.bfloat16) for height in heights],
        scratch_shapes=[pltpu.VMEM((chips * block, 2 * depth), jnp.bfloat16)],
        compiler_params=pltpu.CompilerParams(vmem_limit_bytes=VMEM_LIMIT),
        cost_estimate=FREE,
        name="project",
    )(own, crossed, w_own, w_crossed)


def join_kernel(*refs):
    half = refs[0].shape[0] // 2
    for k, ref in enumerate(refs[:-2]):
        refs[-2][k * half : (k + 1) * half, :] = ref[:half, :]
        refs[-1][k * half : (k + 1) * half, :] = ref[half:, :]


def join(pieces):
    rows, cols = pieces[0].shape
    out = jax.ShapeDtypeStruct((len(pieces) * rows // 2, cols), pieces[0].dtype)
    return pl.pallas_call(
        join_kernel,
        out_shape=[out, out],
        compiler_params=pltpu.CompilerParams(vmem_limit_bytes=VMEM_LIMIT),
        cost_estimate=FREE,
        name="join",
    )(*pieces)


def student_kernel(
    x_ref, own_ref, la_ref, ha_ref, residual_ref, hot_ref, table_ref, head_ref, guided_ref,
    first_ref, second_ref, third_ref, fourth_ref, in_ref, kept_ref, resid_ref,
    stream_ref, normed_ref, dn_ref, dproj_ref,
):
    rows, width = residual_ref.shape
    chunks = table_ref.shape[0] // 2
    cols = width // chunks
    f32 = jnp.float32
    total = jnp.zeros((rows, 1), f32)
    for i in range(chunks):
        part = slice(i * cols, (i + 1) * cols)
        low, high = la_ref[:, part].astype(f32), ha_ref[:, part].astype(f32)
        base = residual_ref[:, part].astype(f32) + own_ref[:, part].astype(f32)
        stream = base + jnp.concatenate([low, high], axis=0)
        stream_ref[:, part] = stream
        total += jnp.sum(stream, axis=-1, keepdims=True)
    mean = total / width
    square = jnp.zeros((rows, 1), f32)
    for i in range(chunks):
        part = slice(i * cols, (i + 1) * cols)
        center = stream_ref[:, part] - mean
        square += jnp.sum(center * center, axis=-1, keepdims=True)
    inverse = lax.rsqrt(square / width + 1e-06)
    hot = hot_ref[...]
    velocity = jnp.zeros((rows, head_ref.shape[0]), f32)
    for i in range(chunks):
        part = slice(i * cols, (i + 1) * cols)
        normed = (stream_ref[:, part] - mean) * inverse
        shift = dot_f32(hot, table_ref[i], 1, 0)
        scale = 1.0 + dot_f32(hot, table_ref[chunks + i], 1, 0)
        model_in = (normed * scale + shift).astype(jnp.bfloat16)
        normed_ref[:, part] = normed
        kept_ref[:, part] = normed.astype(jnp.bfloat16)
        dn_ref[:, part] = scale
        in_ref[:, part] = model_in
        velocity += dot_f32(model_in, head_ref[:, part], 1, 1)
    scale_back = 1.0 / math.sqrt(16384)
    resid = ((velocity - guided_ref[...]) * scale_back).astype(jnp.bfloat16)
    resid_ref[...] = resid
    first = jnp.zeros((rows, 1), f32)
    second = jnp.zeros((rows, 1), f32)
    for i in range(chunks):
        part = slice(i * cols, (i + 1) * cols)
        cotangent = dot_f32(resid, head_ref[:, part], 1, 0)
        normed = normed_ref[:, part]
        dnorm = cotangent * dn_ref[:, part]
        dn_ref[:, part] = dnorm
        first += jnp.sum(dnorm, axis=-1, keepdims=True)
        second += jnp.sum(dnorm * normed, axis=-1, keepdims=True)
    first = first / width
    second = second / width

    def back(chunk):
        part = slice(chunk * cols, (chunk + 1) * cols)
        return inverse * (dn_ref[:, part] - first - normed_ref[:, part] * second)

    side = cols // 2
    for lo in range(2):
        for y in range(0, 4, 2):
            even, odd = back(2 * y + lo), back(2 * y + 2 + lo)
            for hi in range(2):
                cut = slice(hi * side, (hi + 1) * side)
                both = jnp.concatenate([even[:, cut], odd[:, cut]], axis=1)
                dproj_ref[hi * 2 + lo, :, (y // 2) * cols : (y // 2 + 1) * cols] = both.astype(jnp.bfloat16)
    for apart, ref in enumerate((first_ref, second_ref, third_ref, fourth_ref)):
        ref[...] = dproj_ref[lax.rem(x_ref[0] + 4 + x_ref[1] * apart, 4)]

def student(chip_x, own, received, residual, hot, table, head, guided):
    rows, width = residual.shape
    quarter = width // 4
    arrays = (own, *received, residual, hot, table, head, guided)
    outs = [(rows, quarter)] * 4 + [(rows, width), (rows, width), guided.shape]
    return pl.pallas_call(
        student_kernel,
        grid_spec=pltpu.PrefetchScalarGridSpec(
            num_scalar_prefetch=1,
            grid=(1,),
            in_specs=[
                pl.BlockSpec(array.shape, functools.partial(lambda dims, i, p: (0,) * dims, array.ndim))
                for array in arrays
            ],
            out_specs=[pl.BlockSpec(out, lambda i, p: (0, 0)) for out in outs],
            scratch_shapes=[
                pltpu.VMEM((rows, width), jnp.float32),
                pltpu.VMEM((rows, width), jnp.float32),
                pltpu.VMEM((rows, width), jnp.float32),
                pltpu.VMEM((4, rows, quarter), jnp.bfloat16),
            ],
        ),
        out_shape=[jax.ShapeDtypeStruct(out, jnp.bfloat16) for out in outs],
        compiler_params=pltpu.CompilerParams(vmem_limit_bytes=VMEM_LIMIT),
        cost_estimate=FREE,
        name="student",
    )(chip_x, *arrays)


def sums_kernel(
    place_ref, in_ref, normed_ref, resid_ref, hot_ref, head_ref, own_ref, cross_ref, headpart_ref, mod_ref, out_ref
):
    f32, bf16 = jnp.float32, jnp.bfloat16
    chunks, cols, patch = headpart_ref.shape
    samples = mod_ref.shape[1]
    resid = resid_ref[...]
    hot = hot_ref[:, hot_ref.shape[1] - samples :]
    for i in range(chunks):
        part = slice(i * cols, (i + 1) * cols)
        cotangent = dot_f32(resid, head_ref[:, part], 1, 0)
        headpart_ref[i] = dot_f32(in_ref[:, part], resid, 0, 0)
        mod_ref[i] = dot_f32(hot, cotangent.astype(bf16), 0, 0)
        scaled = cotangent * normed_ref[:, part].astype(f32)
        mod_ref[chunks + i] = dot_f32(hot, scaled.astype(bf16), 0, 0)
    strip = cols // (2 * chunks)
    blank = jnp.zeros((strip, cols - chunks * patch), f32)
    for i in range(2 * chunks):
        take = slice(i * strip, (i + 1) * strip)
        head_rows = jnp.concatenate([headpart_ref[k, take, :] for k in range(chunks)] + [blank], axis=1)
        out_ref[i] = jnp.concatenate([head_rows, mod_ref[i]], axis=0).astype(bf16)
    for core, ref in enumerate((own_ref, cross_ref)):
        for pair in range(2):
            for chip in range(4):
                z, c, p = lax.rem(place_ref[0] + chip, 4), lax.rem(place_ref[1] + core, 2), lax.rem(place_ref[2] + pair, 2)
                ref[pair, chip] = out_ref[z * 4 + c * 2 + p]


def local_sums(place, model_in, normed, resid, hot, head, samples, devices):
    rows, width = model_in.shape
    chunk = 2 * width // devices
    part = (chunk // devices + samples, chunk)
    arrays = (model_in, normed, resid, hot, head)
    out = (2, devices // 4) + part
    return pl.pallas_call(
        sums_kernel,
        grid_spec=pltpu.PrefetchScalarGridSpec(
            num_scalar_prefetch=1,
            grid=(1,),
            in_specs=[pl.BlockSpec(array.shape, lambda i, p: (0, 0)) for array in arrays],
            out_specs=[pl.BlockSpec(out, lambda i, p: (0, 0, 0, 0)) for _ in range(2)],
            scratch_shapes=[
                pltpu.VMEM((devices // 2, chunk, head.shape[0]), jnp.float32),
                pltpu.VMEM((devices, samples, chunk), jnp.float32),
                pltpu.VMEM((devices,) + part, jnp.bfloat16),
            ],
        ),
        out_shape=[jax.ShapeDtypeStruct(out, jnp.bfloat16) for _ in range(2)],
        compiler_params=pltpu.CompilerParams(vmem_limit_bytes=VMEM_LIMIT),
        cost_estimate=FREE,
        name="local_sums",
    )(place, *arrays)


def block_rows(refs, position):
    half = 64
    places = (position, position, 2 - position, 2 - position)
    return jnp.concatenate([ref[at * half : (at + 1) * half, :] for ref, at in zip(refs, places)], axis=0)


def early_kernel(*refs):
    out_ref, lefts, refs = refs[-1], refs[:4], refs[4:-1]
    total = jnp.zeros(out_ref.shape, jnp.float32)
    for arrival in range(4):
        rows = jnp.concatenate([refs[0][...], refs[1][...]], axis=0)
        total += dot_f32(lefts[0][arrival], rows, 1, 0)
        refs = refs[2:]
    for arrival in range(3):
        for position in range(3):
            total += dot_f32(lefts[1 + position][arrival], block_rows(refs[:4], position), 1, 0)
        refs = refs[4:]
    out_ref[...] = total


def early_product(lefts, mine, others):
    tile = 256
    flat = [part for blocks in (mine, others) for parts in blocks for part in parts]
    depth, width = lefts[0].shape[1], flat[0].shape[1]
    return pl.pallas_call(
        early_kernel,
        grid=(width // tile,),
        in_specs=[pl.BlockSpec(left.shape, lambda i: (0, 0, 0)) for left in lefts]
        + [pl.BlockSpec((part.shape[0], tile), lambda i: (0, i)) for part in flat],
        out_specs=pl.BlockSpec((depth, tile), lambda i: (0, i)),
        out_shape=jax.ShapeDtypeStruct((depth, width), jnp.float32),
        compiler_params=pltpu.CompilerParams(vmem_limit_bytes=VMEM_LIMIT),
        cost_estimate=FREE,
        name="early_product",
    )(*lefts, *flat)


def late_kernel(y_ref, first_ref, second_ref, third_ref, a_ref, b_ref, c_ref, d_ref, early_ref, *refs):
    outs, turned_ref = refs[:-1], refs[-1]
    step = pl.program_id(0)
    tile = early_ref.shape[1]
    total = early_ref[...]
    for position, left in enumerate((first_ref, second_ref, third_ref)):
        total += dot_f32(left[0], block_rows((a_ref, b_ref, c_ref, d_ref), position), 1, 0)
    turned_ref[pl.ds(pl.multiple_of(step * tile, tile), tile), :] = total.T.astype(jnp.bfloat16)

    @pl.when(step == pl.num_programs(0) - 1)
    def _():
        rows = outs[0].shape[0]
        for apart, out in enumerate(outs):
            start = pl.multiple_of(lax.rem(y_ref[0] + apart, 4) * rows, rows)
            out[...] = turned_ref[pl.ds(start, rows), :]


def late_product(chip_y, lefts, flat, early):
    depth, width = early.shape
    tile = 256
    return pl.pallas_call(
        late_kernel,
        grid_spec=pltpu.PrefetchScalarGridSpec(
            num_scalar_prefetch=1,
            grid=(width // tile,),
            in_specs=[pl.BlockSpec((1,) + left.shape[1:], lambda i, p: (3, 0, 0)) for left in lefts]
            + [pl.BlockSpec((half.shape[0], tile), lambda i, p: (0, i)) for half in flat]
            + [pl.BlockSpec((depth, tile), lambda i, p: (0, i))],
            out_specs=[pl.BlockSpec((width // 4, depth), lambda i, p: (0, 0)) for _ in range(4)],
            scratch_shapes=[pltpu.VMEM((width, depth), jnp.bfloat16)],
        ),
        out_shape=[jax.ShapeDtypeStruct((width // 4, depth), jnp.bfloat16) for _ in range(4)],
        compiler_params=pltpu.CompilerParams(vmem_limit_bytes=VMEM_LIMIT),
        cost_estimate=FREE,
        name="late_product",
    )(chip_y, *lefts, *flat, early)


def local(
    teacher_hidden,
    student_query,
    student_key,
    student_value,
    residual,
    segment_ids,
    timesteps,
    guide_scales,
    time_proj,
    guide_proj,
    teach_head,
    stud_head,
    out_proj,
):
    bf16, f32 = jnp.bfloat16, jnp.float32
    seq_pos, pair_pos, data_pos = lax.axis_index("seq"), lax.axis_index("pair"), lax.axis_index("dp")
    chip_z, core = seq_pos // 2, seq_pos % 2
    chip_y, chip_x = data_pos // 2, pair_pos * 2 + data_pos % 2
    segment = segment_ids[0]
    samples = timesteps.shape[1]
    freq = time_proj.shape[0]

    guidance = guide_scales[0].astype(f32) / 8.0
    t_emb = sinusoid(timesteps[0].astype(f32), freq).astype(bf16)
    g_emb = sinusoid(1000.0 * guidance, freq).astype(bf16)
    teach_cols = jnp.dot(t_emb, time_proj, preferred_element_type=f32)
    stud_cols = teach_cols + jnp.dot(g_emb, guide_proj, preferred_element_type=f32)
    columns = jnp.concatenate([teach_cols, stud_cols], axis=0).astype(bf16)

    stud_rows = student_query.shape[1]
    ids = jnp.arange(2 * samples, dtype=jnp.int32)[None, :]
    hidden = teacher_hidden[0, 0]
    teach_seg = lax.dynamic_slice_in_dim(segment, seq_pos * hidden.shape[0], hidden.shape[0])
    stud_seg = lax.dynamic_slice_in_dim(teach_seg, pair_pos * stud_rows, stud_rows)
    teach_hot = (teach_seg[:, None] == ids).astype(bf16)
    stud_hot = (stud_seg[:, None] == ids - samples).astype(bf16)
    guide_tok = jnp.sum(
        jnp.where(stud_seg[:, None] == ids[:, :samples], guidance[None, :], 0.0), axis=1, keepdims=True
    )

    by_block = segment.reshape(8, 2, stud_rows)
    own_seg = lax.dynamic_index_in_dim(by_block, pair_pos, 1, keepdims=False)
    other_seg = lax.dynamic_index_in_dim(by_block, 1 - pair_pos, 1, keepdims=False)
    turn = jnp.arange(8, dtype=jnp.int32)
    away = ((1 - 2 * core) * (1 - 2 * (turn // 4)) * (turn % 4) + 4) % 4
    spots = (chip_z + away) % 4 * 2 + (core + turn // 4) % 2
    query_seg = own_seg[spots]
    low = jnp.sum((segment[None, :] < query_seg[:, :1]).astype(jnp.int32), axis=1) // 256
    high = (jnp.sum((segment[None, :] <= query_seg[:, -1:]).astype(jnp.int32), axis=1) + 255) // 256
    segs = query_seg[:, :, None], jnp.concatenate([own_seg, other_seg], axis=1)[:, None, :]

    key_crossed, weights_crossed = pair_swap(student_key[0]), core_swap(out_proj)
    first = exchange([student_value[0], student_query[0]], columns)
    first, key_crossed = lax.optimization_barrier((first, key_crossed))
    table = take_rows(first, 2 * stud_rows, columns.shape[0])
    table_other = pair_swap(table)
    value_own, table_other = lax.optimization_barrier((take_rows(first, 0, stud_rows), table_other))
    value_other = pair_swap(value_own)
    second = exchange([student_key[0], key_crossed])
    lower, upper = jnp.where(pair_pos == 0, table, table_other), jnp.where(pair_pos == 0, table_other, table)
    table = jnp.stack([lower, upper], axis=1).reshape((16,) + columns.shape)
    velocity = teacher(hidden, teach_hot, table, teach_head.T)
    own_vel = lax.dynamic_slice_in_dim(velocity, pair_pos * stud_rows, stud_rows, 0)
    sent_vel = lax.dynamic_slice_in_dim(velocity, (1 - pair_pos) * stud_rows, stud_rows, 0)
    value_other, second, weights_crossed, low, high, segs, sent_vel = lax.optimization_barrier(
        (value_other, second, weights_crossed, low, high, segs, sent_vel)
    )
    attn_own, attn_cross, turned = attend(
        low, high, spots, *segs, value_other, first, second
    )

    own, *terms = project(attn_own, core_swap(attn_cross), out_proj, weights_crossed)
    received = ring_reduce(terms[4::-2], terms[5::-2])
    lefts = [turned]
    for _ in range(2):
        lefts.append(x_shift(lefts[-1], 1))
    other_vel = pair_swap(sent_vel.astype(bf16)).astype(f32)
    cond_vel = jnp.where(pair_pos == 0, own_vel, other_vel)
    uncond_vel = jnp.where(pair_pos == 0, other_vel, own_vel)
    guided = uncond_vel + guide_tok * (cond_vel - uncond_vel)
    own, lefts[1:3], guided = lax.optimization_barrier((own, lefts[1:3], guided))

    x_at = jnp.stack([chip_x, 1 - 2 * core]).astype(jnp.int32)
    y_at = jnp.reshape(chip_y, (1,)).astype(jnp.int32)
    *quarters, model_in, normed, resid = student(
        x_at, own, received, residual[0], stud_hot, table, stud_head.T, guided
    )

    from_x = [x_shift(quarters[apart], apart) for apart in (1, 2, 3)]
    mine = [quarters[0], seq_ring(quarters[0])]
    at = jnp.stack([chip_z, core, pair_pos]).astype(jnp.int32)
    kept, sent = local_sums(at, model_in, normed, resid, stud_hot, stud_head.T, samples, table.shape[0])
    from_x, kept, sent, mine[1] = lax.optimization_barrier((from_x, kept, sent, mine[1]))
    for _ in range(2):
        mine.append(seq_ring(mine[-1]))
    mine = [(block, core_swap(block)) for block in mine]
    came = core_swap(sent)
    kept, sent = add_rows(kept[0], came[0]), add_rows(kept[1], came[1])
    came = pair_swap(sent)
    came, lefts[2] = lax.optimization_barrier((came, lefts[2]))
    lefts.append(x_shift(lefts[2], 1))
    others = list(zip(*[ring_gather(half) for half in join(from_x)]))
    kept = add_rows(kept, came)
    sums = kept[0].astype(f32)
    for apart in (1, 2, 3):
        sums = sums + seq_shift(kept[apart], apart).astype(f32)
    sums = sums.astype(bf16)
    others_crossed = [tuple(core_swap(half) for half in pair) for pair in others[:3]]
    early = early_product(lefts, mine, [own + crossed for own, crossed in zip(others, others_crossed)])
    early, last = lax.optimization_barrier((early, others[3]))
    product = late_product(y_at, lefts[1:], [*last, *[core_swap(half) for half in last]], early)

    strip, patch, cols = sums.shape[0] - samples, stud_head.shape[1], sums.shape[1]
    head_sums = sums[:strip, : 8 * patch].reshape(strip, 8, patch).transpose(1, 0, 2)
    d_mod = jnp.broadcast_to(sums[None, strip:], (8, samples, cols))
    emb = g_emb.reshape(samples, 8, freq // 8).transpose(1, 0, 2)
    sent = jnp.concatenate(
        [
            jnp.pad(head_sums, ((0, 0), (0, 0), (0, 128 - patch))),
            jnp.pad(d_mod, ((0, 0), (0, strip - samples), (0, 0))),
            jnp.pad(emb, ((0, 0), (0, strip - samples), (0, 128 - freq // 8))),
        ],
        axis=2,
    )
    got = lax.all_to_all(sent, "dp", 0, 0, tiled=True)
    grad_head = jnp.sum(got[:, :, :patch].astype(f32), axis=0)
    d_mods = got[:, :samples, 128 : 128 + cols].reshape(8 * samples, cols)
    embs = got[:, :samples, 128 + cols : 128 + cols + freq // 8].reshape(8 * samples, freq // 8)
    grad_guidance = dot_f32(embs, d_mods, 0, 0)

    total = product[0].astype(f32)
    for apart in (2, 1, 3):
        total = total + y_shift(product[apart], apart).astype(f32)
    grad_out_proj = total.T
    return (grad_out_proj, grad_head, grad_guidance)


def solution(mesh):
    placed = (
        P("pair", "dp", "seq", None),
        P("dp", ("seq", "pair"), None),
        P("dp", ("seq", "pair"), None),
        P("dp", ("seq", "pair"), None),
        P("dp", ("seq", "pair"), None),
        P("dp", None),
        P("dp", None),
        P("dp", None),
        P(None, ("seq", "pair")),
        P(None, ("seq", "pair")),
        P(),
        P(),
        P("seq", None),
    )
    return jax.shard_map(
        local,
        mesh=mesh,
        in_specs=placed,
        out_specs=(
            P("seq", ("dp", "pair")),
            P(("dp", "seq", "pair"), None),
            P("dp", ("seq", "pair")),
        ),
        check_vma=False,
    )
```

```python
import functools
import math

import jax
import jax.numpy as jnp
from jax import lax
from jax.experimental import pallas as pl
from jax.experimental.pallas import tpu as pltpu
from jax.sharding import PartitionSpec as P

HEAD_DIM = 128
VMEM_LIMIT = 56 * 1024 * 1024
FREE = pl.CostEstimate(flops=0, bytes_accessed=0, transcendentals=0)


def side(core):
    return 1 if core == 0 else -1


def seq_shift(value, apart):
    return lax.ppermute(value, "seq", [(i, ((i // 2 + apart) % 4) * 2 + i % 2) for i in range(8)])


def seq_ring(value):
    return lax.ppermute(value, "seq", [(i, ((i // 2 + side(i % 2)) % 4) * 2 + i % 2) for i in range(8)])


def core_swap(value):
    return lax.ppermute(value, "seq", [(i, i ^ 1) for i in range(8)])


def y_shift(value, apart):
    return lax.ppermute(value, "dp", [(i, ((i // 2 + apart) % 4) * 2 + i % 2) for i in range(8)])


def x_shift(value, apart):
    def target(index):
        data, seq, pair = index // 16, index // 2 % 8, index % 2
        x = (pair * 2 + data % 2 + side(seq % 2) * apart) % 4
        return (data // 2 * 2 + x % 2) * 16 + seq * 2 + x // 2

    return lax.ppermute(value, ("dp", "seq", "pair"), [(i, target(i)) for i in range(128)])


def pair_swap(value):
    return lax.ppermute(value, "pair", [(0, 1), (1, 0)])


def add_rows(left, right):
    return (left.astype(jnp.float32) + right.astype(jnp.float32)).astype(jnp.bfloat16)


def ring_reduce(low, high):
    totals = [seq_ring(low[0]), seq_ring(high[0])]
    for terms in zip(low[1:], high[1:]):
        totals = [seq_ring(add_rows(term, total)) for term, total in zip(terms, totals)]
    return totals


def ring_gather(block):
    blocks = [block]
    for _ in range(3):
        blocks.append(seq_ring(blocks[-1]))
    return blocks


def sinusoid(values, width):
    half = width // 2
    steps = jnp.arange(half, dtype=jnp.float32)
    freqs = jnp.exp(-math.log(10000.0) * steps / half)
    angles = values[..., None] * freqs
    return jnp.concatenate([jnp.cos(angles), jnp.sin(angles)], axis=-1)


def dot_f32(left, right, left_dim, right_dim):
    return lax.dot_general(
        left, right, (((left_dim,), (right_dim,)), ((), ())), preferred_element_type=jnp.float32
    )


def teacher_kernel(hidden_ref, hot_ref, table_ref, head_ref, out_ref):
    rows, width = hidden_ref.shape
    chunks = table_ref.shape[0] // 2
    cols = width // chunks
    hidden = hidden_ref[...].astype(jnp.float32)
    center = hidden - jnp.mean(hidden, axis=-1, keepdims=True)
    inverse = lax.rsqrt(jnp.mean(center * center, axis=-1, keepdims=True) + 1e-06)
    hot = hot_ref[...]
    total = jnp.zeros((rows, head_ref.shape[0]), jnp.float32)
    for i in range(chunks):
        part = slice(i * cols, (i + 1) * cols)
        shift = dot_f32(hot, table_ref[i], 1, 0)
        scale = dot_f32(hot, table_ref[chunks + i], 1, 0)
        normed = center[:, part] * inverse
        model_in = (normed * (1.0 + scale) + shift).astype(jnp.bfloat16)
        total += dot_f32(model_in, head_ref[:, part], 1, 1)
    out_ref[...] = total


def teacher(hidden, hot, table, head):
    rows, width = hidden.shape
    block = 128
    patch = head.shape[0]
    return pl.pallas_call(
        teacher_kernel,
        grid=(rows // block,),
        in_specs=[
            pl.BlockSpec((block, width), lambda i: (i, 0)),
            pl.BlockSpec((block, hot.shape[1]), lambda i: (i, 0)),
            pl.BlockSpec(table.shape, lambda i: (0, 0, 0)),
            pl.BlockSpec(head.shape, lambda i: (0, 0)),
        ],
        out_specs=pl.BlockSpec((block, patch), lambda i: (i, 0)),
        out_shape=jax.ShapeDtypeStruct((rows, patch), jnp.float32),
        compiler_params=pltpu.CompilerParams(vmem_limit_bytes=VMEM_LIMIT),
        cost_estimate=FREE,
        name="teacher",
    )(hidden, hot, table, head)


def pack_kernel(tensors, *refs):
    out_ref = refs[-1]
    groups = out_ref.shape[0]
    for g in range(groups):
        start = 0
        for ref in [refs[t * groups + g] for t in range(tensors)] + list(refs[tensors * groups : -1]):
            out_ref[g, start : start + ref.shape[0]] = ref[...]
            start += ref.shape[0]


def exchange(tensors, *shared):
    rows, width = tensors[0].shape
    groups, count = 8, len(tensors)
    cols = width // groups
    half = groups // 2
    height = count * rows + sum(array.shape[0] for array in shared)
    packed = pl.pallas_call(
        functools.partial(pack_kernel, count),
        grid=(2,),
        in_specs=[
            pl.BlockSpec((rows, cols), functools.partial(lambda g, i: (0, i * half + g), g))
            for _ in tensors
            for g in range(half)
        ]
        + [pl.BlockSpec(array.shape, lambda i: (0, 0)) for array in shared],
        out_specs=pl.BlockSpec((half, height, cols), lambda i: (i, 0, 0)),
        out_shape=jax.ShapeDtypeStruct((groups, height, cols), tensors[0].dtype),
        compiler_params=pltpu.CompilerParams(vmem_limit_bytes=VMEM_LIMIT),
        cost_estimate=FREE,
        name="pack",
    )(*[tensor for tensor in tensors for _ in range(half)], *shared)
    return lax.all_to_all(packed, "seq", 0, 0, tiled=True)


def rows_kernel(*refs):
    half = len(refs) // 2
    for source, out in zip(refs[:half], refs[half:]):
        out[...] = source[...]


def take_rows(pieces, *spans):
    blocks, _, cols = pieces.shape
    half = blocks // 2
    return pl.pallas_call(
        rows_kernel,
        grid=(2,),
        in_specs=[
            pl.BlockSpec((half, rows, cols), functools.partial(lambda at, i: (i, at, 0), start // rows))
            for start, rows in spans
        ],
        out_specs=[pl.BlockSpec((half, rows, cols), lambda i: (i, 0, 0)) for _, rows in spans],
        out_shape=[jax.ShapeDtypeStruct((blocks, rows, cols), pieces.dtype) for _, rows in spans],
        compiler_params=pltpu.CompilerParams(vmem_limit_bytes=16 * 1024 * 1024),
        cost_estimate=FREE,
        name="take_rows",
    )(*[pieces for _ in spans])


def attend_kernel(
    low_ref, high_ref, turn_ref, qseg_ref, kseg_ref, value_ref, first_ref, second_ref,
    out_ref, cross_ref, turned_ref, score_ref, top_ref, acc_ref,
):
    block = value_ref.shape[1]
    heads = value_ref.shape[2] // HEAD_DIM
    upper, lower = slice(0, block), slice(block, 2 * block)
    step = pl.program_id(0)
    low, high = low_ref[step], high_ref[step]
    factor = math.log2(math.e) / math.sqrt(HEAD_DIM)
    parts = [slice(h * HEAD_DIM, (h + 1) * HEAD_DIM) for h in range(heads)]
    top_ref[...] = jnp.full_like(top_ref, -1e30)
    acc_ref[...] = jnp.zeros_like(acc_ref)
    query_seg = qseg_ref[0]

    def score(index, carry):
        same = query_seg == kseg_ref[index]
        scores = [
            dot_f32(first_ref[turn_ref[step], lower, part], second_ref[index, :, part], 1, 1) for part in parts
        ]
        for h in range(heads):
            masked = jnp.where(same, scores[h] * factor, -1e30)
            score_ref[index - low, h] = masked
            pair = jnp.maximum(masked[:, :block], masked[:, block:])
            top_ref[h] = jnp.maximum(top_ref[h], pair)
        return carry

    lax.fori_loop(low, high, score, 0)
    for h in range(heads):
        top_ref[h] = jnp.broadcast_to(jnp.max(top_ref[h], axis=-1, keepdims=True), top_ref.shape[1:])
    ones = jnp.ones((2 * block, HEAD_DIM), jnp.bfloat16)

    def mix(index, carry):
        weights = []
        for h in range(heads):
            top = jnp.concatenate([top_ref[h], top_ref[h]], axis=1)
            weights.append(jnp.exp2(score_ref[index - low, h] - top).astype(jnp.bfloat16))
        for h, part in enumerate(parts):
            values = jnp.concatenate([first_ref[index, upper, part], value_ref[index, :, part]], axis=0)
            acc_ref[h] += dot_f32(weights[h], jnp.concatenate([values, ones], axis=1), 1, 0)
        return carry

    lax.fori_loop(low, high, mix, 0)
    result = jnp.concatenate(
        [acc_ref[h, :, :HEAD_DIM] / acc_ref[h, :, HEAD_DIM:] for h in range(heads)], axis=1
    )
    rounded = result.astype(jnp.bfloat16)

    @pl.when(step < 4)
    def _():
        out_ref[0] = rounded

    @pl.when(step >= 4)
    def _():
        cross_ref[0] = rounded

    turned = result.T.astype(jnp.bfloat16)
    arrival = lax.rem(8 - step, 4)
    for core in range(2):

        @pl.when(step // 4 == core)
        def _():
            turned_ref[arrival, :, core * block : (core + 1) * block] = turned


def attend(low, high, turn, query_seg, key_seg, value_other, first, second):
    blocks, block, width = value_other.shape
    chips = blocks // 2
    heads = width // HEAD_DIM

    def fixed(array):
        return pl.BlockSpec(array.shape, lambda j, *_: (0,) * array.ndim, pipeline_mode=pl.Buffered(1))

    return pl.pallas_call(
        attend_kernel,
        grid_spec=pltpu.PrefetchScalarGridSpec(
            num_scalar_prefetch=3,
            grid=(blocks,),
            in_specs=[pl.BlockSpec((1, block, 1), lambda j, *_: (j, 0, 0))]
            + [fixed(array) for array in (key_seg, value_other, first, second)],
            out_specs=[
                pl.BlockSpec((1, block, width), lambda j, *_: (jnp.minimum(j, 3), 0, 0)),
                pl.BlockSpec((1, block, width), lambda j, *_: (jnp.maximum(j - 4, 0), 0, 0)),
                pl.BlockSpec((chips, width, 2 * block), lambda j, *_: (0, 0, 0)),
            ],
            scratch_shapes=[
                pltpu.VMEM((6, heads, block, 2 * block), jnp.float32),
                pltpu.VMEM((heads, block, block), jnp.float32),
                pltpu.VMEM((heads, block, 2 * HEAD_DIM), jnp.float32),
            ],
        ),
        out_shape=[
            jax.ShapeDtypeStruct((chips, block, width), jnp.bfloat16),
            jax.ShapeDtypeStruct((chips, block, width), jnp.bfloat16),
            jax.ShapeDtypeStruct((chips, width, 2 * block), jnp.bfloat16),
        ],
        compiler_params=pltpu.CompilerParams(vmem_limit_bytes=24 * 1024 * 1024),
        cost_estimate=FREE,
        name="attend",
    )(low, high, turn, query_seg, key_seg, value_other, first, second)


def project_kernel(own_ref, crossed_ref, w_own_ref, w_crossed_ref, *refs):
    outs, left_ref = refs[:-1], refs[-1]
    chips, block, depth = own_ref.shape

    @pl.when(pl.program_id(0) == 0)
    def _():
        for k in range(chips):
            take, even = slice(k * block, (k + 1) * block), depth // 256 * 256
            left_ref[take, :even] = own_ref[k, :, :even]
            left_ref[take, even : 2 * even] = crossed_ref[k, :, :even]
            left_ref[take, 2 * even : depth + even] = own_ref[k, :, even:]
            left_ref[take, depth + even :] = crossed_ref[k, :, even:]

    even = depth // 256 * 256
    rest = jnp.concatenate([w_own_ref[even:, :], w_crossed_ref[even:, :]], axis=0)
    total = dot_f32(left_ref[:, :even], w_own_ref[:even, :], 1, 0)
    total += dot_f32(left_ref[:, even : 2 * even], w_crossed_ref[:even, :], 1, 0)
    total = (total + dot_f32(left_ref[:, 2 * even :], rest, 1, 0)).astype(jnp.bfloat16)
    start = 0
    for out in outs:
        out[...] = total[start : start + out.shape[0]]
        start += out.shape[0]


def project(own, crossed, w_own, w_crossed):
    chips, block, depth = own.shape
    width = w_own.shape[1]
    tile = 1024
    heights = [block] + [block // 2] * (2 * chips - 2)
    left = pl.BlockSpec(own.shape, lambda i: (0, 0, 0))
    right = pl.BlockSpec((depth, tile), lambda i: (0, i))
    return pl.pallas_call(
        project_kernel,
        grid=(width // tile,),
        in_specs=[left, left, right, right],
        out_specs=[pl.BlockSpec((height, tile), lambda i: (0, i)) for height in heights],
        out_shape=[jax.ShapeDtypeStruct((height, width), jnp.bfloat16) for height in heights],
        scratch_shapes=[pltpu.VMEM((chips * block, 2 * depth), jnp.bfloat16)],
        compiler_params=pltpu.CompilerParams(vmem_limit_bytes=VMEM_LIMIT),
        cost_estimate=FREE,
        name="project",
    )(own, crossed, w_own, w_crossed)


def join_kernel(*refs):
    half = refs[0].shape[0] // 2
    for k, ref in enumerate(refs[:-2]):
        refs[-2][k * half : (k + 1) * half, :] = ref[:half, :]
        refs[-1][k * half : (k + 1) * half, :] = ref[half:, :]


def join(pieces):
    rows, cols = pieces[0].shape
    out = jax.ShapeDtypeStruct((len(pieces) * rows // 2, cols), pieces[0].dtype)
    return pl.pallas_call(
        join_kernel,
        out_shape=[out, out],
        compiler_params=pltpu.CompilerParams(vmem_limit_bytes=16 * 1024 * 1024),
        cost_estimate=FREE,
        name="join",
    )(*pieces)


def student_kernel(
    x_ref, own_ref, la_ref, ha_ref, residual_ref, hot_ref, table_ref, head_ref, guided_ref,
    first_ref, second_ref, third_ref, fourth_ref, in_ref, kept_ref, resid_ref,
    stream_ref, normed_ref, dn_ref, dproj_ref,
):
    rows, width = residual_ref.shape
    chunks = table_ref.shape[0] // 2
    cols = width // chunks
    f32 = jnp.float32
    total = jnp.zeros((rows, 1), f32)
    for i in range(chunks):
        part = slice(i * cols, (i + 1) * cols)
        low, high = la_ref[:, part].astype(f32), ha_ref[:, part].astype(f32)
        base = residual_ref[:, part].astype(f32) + own_ref[:, part].astype(f32)
        stream = base + jnp.concatenate([low, high], axis=0)
        stream_ref[:, part] = stream
        total += jnp.sum(stream, axis=-1, keepdims=True)
    mean = total / width
    square = jnp.zeros((rows, 1), f32)
    for i in range(chunks):
        part = slice(i * cols, (i + 1) * cols)
        center = stream_ref[:, part] - mean
        square += jnp.sum(center * center, axis=-1, keepdims=True)
    inverse = lax.rsqrt(square / width + 1e-06)
    hot = hot_ref[...]
    velocity = jnp.zeros((rows, head_ref.shape[0]), f32)
    for i in range(chunks):
        part = slice(i * cols, (i + 1) * cols)
        normed = (stream_ref[:, part] - mean) * inverse
        shift = dot_f32(hot, table_ref[i], 1, 0)
        scale = 1.0 + dot_f32(hot, table_ref[chunks + i], 1, 0)
        model_in = (normed * scale + shift).astype(jnp.bfloat16)
        normed_ref[:, part] = normed
        kept_ref[:, part] = normed.astype(jnp.bfloat16)
        dn_ref[:, part] = scale
        in_ref[:, part] = model_in
        velocity += dot_f32(model_in, head_ref[:, part], 1, 1)
    scale_back = 1.0 / math.sqrt(16384)
    resid = ((velocity - guided_ref[...]) * scale_back).astype(jnp.bfloat16)
    resid_ref[...] = resid
    first = jnp.zeros((rows, 1), f32)
    second = jnp.zeros((rows, 1), f32)
    for i in range(chunks):
        part = slice(i * cols, (i + 1) * cols)
        cotangent = dot_f32(resid, head_ref[:, part], 1, 0)
        normed = normed_ref[:, part]
        dnorm = cotangent * dn_ref[:, part]
        dn_ref[:, part] = dnorm
        first += jnp.sum(dnorm, axis=-1, keepdims=True)
        second += jnp.sum(dnorm * normed, axis=-1, keepdims=True)
    first = first / width
    second = second / width

    def back(chunk):
        part = slice(chunk * cols, (chunk + 1) * cols)
        return inverse * (dn_ref[:, part] - first - normed_ref[:, part] * second)

    side = cols // 2
    for lo in range(2):
        for y in range(0, 4, 2):
            even, odd = back(2 * y + lo), back(2 * y + 2 + lo)
            for hi in range(2):
                cut = slice(hi * side, (hi + 1) * side)
                both = jnp.concatenate([even[:, cut], odd[:, cut]], axis=1)
                dproj_ref[hi * 2 + lo, :, (y // 2) * cols : (y // 2 + 1) * cols] = both.astype(jnp.bfloat16)
    for apart, ref in enumerate((first_ref, second_ref, third_ref, fourth_ref)):
        ref[...] = dproj_ref[lax.rem(x_ref[0] + 4 + x_ref[1] * apart, 4)]

def student(chip_x, own, received, residual, hot, table, head, guided):
    rows, width = residual.shape
    quarter = width // 4
    arrays = (own, *received, residual, hot, table, head, guided)
    outs = [(rows, quarter)] * 4 + [(rows, width), (rows, width), guided.shape]
    return pl.pallas_call(
        student_kernel,
        grid_spec=pltpu.PrefetchScalarGridSpec(
            num_scalar_prefetch=1,
            grid=(1,),
            in_specs=[
                pl.BlockSpec(array.shape, functools.partial(lambda dims, i, p: (0,) * dims, array.ndim))
                for array in arrays
            ],
            out_specs=[pl.BlockSpec(out, lambda i, p: (0, 0)) for out in outs],
            scratch_shapes=[
                pltpu.VMEM((rows, width), jnp.float32),
                pltpu.VMEM((rows, width), jnp.float32),
                pltpu.VMEM((rows, width), jnp.float32),
                pltpu.VMEM((4, rows, quarter), jnp.bfloat16),
            ],
        ),
        out_shape=[jax.ShapeDtypeStruct(out, jnp.bfloat16) for out in outs],
        compiler_params=pltpu.CompilerParams(vmem_limit_bytes=40 * 1024 * 1024),
        cost_estimate=FREE,
        name="student",
    )(chip_x, *arrays)


def sums_kernel(
    place_ref, in_ref, normed_ref, resid_ref, hot_ref, head_ref, own_ref, cross_ref, headpart_ref, mod_ref, out_ref
):
    f32, bf16 = jnp.float32, jnp.bfloat16
    chunks, cols, patch = headpart_ref.shape
    samples = mod_ref.shape[1]
    resid = resid_ref[...]
    hot = hot_ref[:, hot_ref.shape[1] - samples :]
    for i in range(chunks):
        part = slice(i * cols, (i + 1) * cols)
        cotangent = dot_f32(resid, head_ref[:, part], 1, 0)
        headpart_ref[i] = dot_f32(in_ref[:, part], resid, 0, 0)
        mod_ref[i] = dot_f32(hot, cotangent.astype(bf16), 0, 0)
        scaled = cotangent * normed_ref[:, part].astype(f32)
        mod_ref[chunks + i] = dot_f32(hot, scaled.astype(bf16), 0, 0)
    strip = cols // (2 * chunks)
    blank = jnp.zeros((strip, cols - chunks * patch), f32)
    for i in range(2 * chunks):
        take = slice(i * strip, (i + 1) * strip)
        head_rows = jnp.concatenate([headpart_ref[k, take, :] for k in range(chunks)] + [blank], axis=1)
        out_ref[i] = jnp.concatenate([head_rows, mod_ref[i]], axis=0).astype(bf16)
    for core, ref in enumerate((own_ref, cross_ref)):
        for pair in range(2):
            for chip in range(4):
                z, c, p = lax.rem(place_ref[0] + chip, 4), lax.rem(place_ref[1] + core, 2), lax.rem(place_ref[2] + pair, 2)
                ref[pair, chip] = out_ref[z * 4 + c * 2 + p]


def local_sums(place, model_in, normed, resid, hot, head, samples, devices):
    rows, width = model_in.shape
    chunk = 2 * width // devices
    part = (chunk // devices + samples, chunk)
    arrays = (model_in, normed, resid, hot, head)
    out = (2, devices // 4) + part
    return pl.pallas_call(
        sums_kernel,
        grid_spec=pltpu.PrefetchScalarGridSpec(
            num_scalar_prefetch=1,
            grid=(1,),
            in_specs=[pl.BlockSpec(array.shape, lambda i, p: (0, 0)) for array in arrays],
            out_specs=[pl.BlockSpec(out, lambda i, p: (0, 0, 0, 0)) for _ in range(2)],
            scratch_shapes=[
                pltpu.VMEM((devices // 2, chunk, head.shape[0]), jnp.float32),
                pltpu.VMEM((devices, samples, chunk), jnp.float32),
                pltpu.VMEM((devices,) + part, jnp.bfloat16),
            ],
        ),
        out_shape=[jax.ShapeDtypeStruct(out, jnp.bfloat16) for _ in range(2)],
        compiler_params=pltpu.CompilerParams(vmem_limit_bytes=24 * 1024 * 1024),
        cost_estimate=FREE,
        name="local_sums",
    )(place, *arrays)


def block_rows(refs, position):
    half = 64
    places = (position, position, 2 - position, 2 - position)
    return jnp.concatenate([ref[at * half : (at + 1) * half, :] for ref, at in zip(refs, places)], axis=0)


def early_kernel(*refs):
    out_ref, lefts, refs = refs[-1], refs[:4], refs[4:-1]
    total = jnp.zeros(out_ref.shape, jnp.float32)
    for arrival in range(4):
        rows = jnp.concatenate([refs[0][...], refs[1][...]], axis=0)
        total += dot_f32(lefts[0][arrival], rows, 1, 0)
        refs = refs[2:]
    for arrival in range(3):
        for position in range(3):
            total += dot_f32(lefts[1 + position][arrival], block_rows(refs[:4], position), 1, 0)
        refs = refs[4:]
    out_ref[...] = total


def early_product(lefts, mine, others):
    tile = 256
    flat = [part for blocks in (mine, others) for parts in blocks for part in parts]
    depth, width = lefts[0].shape[1], flat[0].shape[1]
    return pl.pallas_call(
        early_kernel,
        grid=(width // tile,),
        in_specs=[pl.BlockSpec(left.shape, lambda i: (0, 0, 0)) for left in lefts]
        + [pl.BlockSpec((part.shape[0], tile), lambda i: (0, i)) for part in flat],
        out_specs=pl.BlockSpec((depth, tile), lambda i: (0, i)),
        out_shape=jax.ShapeDtypeStruct((depth, width), jnp.float32),
        compiler_params=pltpu.CompilerParams(vmem_limit_bytes=VMEM_LIMIT),
        cost_estimate=FREE,
        name="early_product",
    )(*lefts, *flat)


def late_kernel(y_ref, first_ref, second_ref, third_ref, a_ref, b_ref, c_ref, d_ref, early_ref, *refs):
    outs, turned_ref = refs[:-1], refs[-1]
    step = pl.program_id(0)
    tile = early_ref.shape[1]
    total = early_ref[...]
    for position, left in enumerate((first_ref, second_ref, third_ref)):
        total += dot_f32(left[0], block_rows((a_ref, b_ref, c_ref, d_ref), position), 1, 0)
    turned_ref[pl.ds(pl.multiple_of(step * tile, tile), tile), :] = total.T.astype(jnp.bfloat16)

    @pl.when(step == pl.num_programs(0) - 1)
    def _():
        rows = outs[0].shape[0]
        for apart, out in enumerate(outs):
            start = pl.multiple_of(lax.rem(y_ref[0] + apart, 4) * rows, rows)
            out[...] = turned_ref[pl.ds(start, rows), :]


def late_product(chip_y, lefts, flat, early):
    depth, width = early.shape
    tile = 256
    return pl.pallas_call(
        late_kernel,
        grid_spec=pltpu.PrefetchScalarGridSpec(
            num_scalar_prefetch=1,
            grid=(width // tile,),
            in_specs=[pl.BlockSpec((1,) + left.shape[1:], lambda i, p: (3, 0, 0)) for left in lefts]
            + [pl.BlockSpec((half.shape[0], tile), lambda i, p: (0, i)) for half in flat]
            + [pl.BlockSpec((depth, tile), lambda i, p: (0, i))],
            out_specs=[pl.BlockSpec((width // 4, depth), lambda i, p: (0, 0)) for _ in range(4)],
            scratch_shapes=[pltpu.VMEM((width, depth), jnp.bfloat16)],
        ),
        out_shape=[jax.ShapeDtypeStruct((width // 4, depth), jnp.bfloat16) for _ in range(4)],
        compiler_params=pltpu.CompilerParams(vmem_limit_bytes=VMEM_LIMIT),
        cost_estimate=FREE,
        name="late_product",
    )(chip_y, *lefts, *flat, early)


def local(
    teacher_hidden,
    student_query,
    student_key,
    student_value,
    residual,
    segment_ids,
    timesteps,
    guide_scales,
    time_proj,
    guide_proj,
    teach_head,
    stud_head,
    out_proj,
):
    bf16, f32 = jnp.bfloat16, jnp.float32
    seq_pos, pair_pos, data_pos = lax.axis_index("seq"), lax.axis_index("pair"), lax.axis_index("dp")
    chip_z, core = seq_pos // 2, seq_pos % 2
    chip_y, chip_x = data_pos // 2, pair_pos * 2 + data_pos % 2
    segment = segment_ids[0]
    samples = timesteps.shape[1]
    freq = time_proj.shape[0]

    guidance = guide_scales[0].astype(f32) / 8.0
    t_emb = sinusoid(timesteps[0].astype(f32), freq).astype(bf16)
    g_emb = sinusoid(1000.0 * guidance, freq).astype(bf16)
    teach_cols = jnp.dot(t_emb, time_proj, preferred_element_type=f32)
    stud_cols = teach_cols + jnp.dot(g_emb, guide_proj, preferred_element_type=f32)
    columns = jnp.concatenate([teach_cols, stud_cols], axis=0).astype(bf16)

    stud_rows = student_query.shape[1]
    ids = jnp.arange(2 * samples, dtype=jnp.int32)[None, :]
    hidden = teacher_hidden[0, 0]
    teach_seg = lax.dynamic_slice_in_dim(segment, seq_pos * hidden.shape[0], hidden.shape[0])
    stud_seg = lax.dynamic_slice_in_dim(teach_seg, pair_pos * stud_rows, stud_rows)
    teach_hot = (teach_seg[:, None] == ids).astype(bf16)
    stud_hot = (stud_seg[:, None] == ids - samples).astype(bf16)
    guide_tok = jnp.sum(
        jnp.where(stud_seg[:, None] == ids[:, :samples], guidance[None, :], 0.0), axis=1, keepdims=True
    )

    by_block = segment.reshape(8, 2, stud_rows)
    own_seg = lax.dynamic_index_in_dim(by_block, pair_pos, 1, keepdims=False)
    other_seg = lax.dynamic_index_in_dim(by_block, 1 - pair_pos, 1, keepdims=False)
    turn = jnp.arange(8, dtype=jnp.int32)
    away = ((1 - 2 * core) * (1 - 2 * (turn // 4)) * (turn % 4) + 4) % 4
    spots = (chip_z + away) % 4 * 2 + (core + turn // 4) % 2
    query_seg = own_seg[spots]
    low = jnp.sum((segment[None, :] < query_seg[:, :1]).astype(jnp.int32), axis=1) // 256
    high = (jnp.sum((segment[None, :] <= query_seg[:, -1:]).astype(jnp.int32), axis=1) + 255) // 256
    segs = query_seg[:, :, None], jnp.concatenate([own_seg, other_seg], axis=1)[:, None, :]

    key_crossed, weights_crossed = pair_swap(student_key[0]), core_swap(out_proj)
    first = exchange([student_value[0], student_query[0]], columns)
    first, key_crossed = lax.optimization_barrier((first, key_crossed))
    value_own, table = take_rows(first, (0, stud_rows), (2 * stud_rows, columns.shape[0]))
    value_own, table_other = lax.optimization_barrier((value_own, pair_swap(table)))
    value_other = pair_swap(value_own)
    second = exchange([student_key[0], key_crossed])
    lower, upper = jnp.where(pair_pos == 0, table, table_other), jnp.where(pair_pos == 0, table_other, table)
    table = jnp.stack([lower, upper], axis=1).reshape((16,) + columns.shape)
    velocity = teacher(hidden, teach_hot, table, teach_head.T)
    own_vel = lax.dynamic_slice_in_dim(velocity, pair_pos * stud_rows, stud_rows, 0)
    sent_vel = lax.dynamic_slice_in_dim(velocity, (1 - pair_pos) * stud_rows, stud_rows, 0)
    value_other, second, weights_crossed, low, high, segs, sent_vel = lax.optimization_barrier(
        (value_other, second, weights_crossed, low, high, segs, sent_vel)
    )
    attn_own, attn_cross, turned = attend(
        low, high, spots, *segs, value_other, first, second
    )

    own, *terms = project(attn_own, core_swap(attn_cross), out_proj, weights_crossed)
    received = ring_reduce(terms[4::-2], terms[5::-2])
    lefts = [turned]
    for _ in range(2):
        lefts.append(x_shift(lefts[-1], 1))
    other_vel = pair_swap(sent_vel.astype(bf16)).astype(f32)
    cond_vel = jnp.where(pair_pos == 0, own_vel, other_vel)
    uncond_vel = jnp.where(pair_pos == 0, other_vel, own_vel)
    guided = uncond_vel + guide_tok * (cond_vel - uncond_vel)
    own, lefts[1:3], guided = lax.optimization_barrier((own, lefts[1:3], guided))

    x_at = jnp.stack([chip_x, 1 - 2 * core]).astype(jnp.int32)
    y_at = jnp.reshape(chip_y, (1,)).astype(jnp.int32)
    *quarters, model_in, normed, resid = student(
        x_at, own, received, residual[0], stud_hot, table, stud_head.T, guided
    )

    from_x = [x_shift(quarters[apart], apart) for apart in (1, 2, 3)]
    mine = [quarters[0], seq_ring(quarters[0])]
    at = jnp.stack([chip_z, core, pair_pos]).astype(jnp.int32)
    kept, sent = local_sums(at, model_in, normed, resid, stud_hot, stud_head.T, samples, table.shape[0])
    from_x, kept, sent, mine[1] = lax.optimization_barrier((from_x, kept, sent, mine[1]))
    for _ in range(2):
        mine.append(seq_ring(mine[-1]))
    mine = [(block, core_swap(block)) for block in mine]
    came = core_swap(sent)
    kept, sent = add_rows(kept[0], came[0]), add_rows(kept[1], came[1])
    came = pair_swap(sent)
    came, lefts[2] = lax.optimization_barrier((came, lefts[2]))
    lefts.append(x_shift(lefts[2], 1))
    others = list(zip(*[ring_gather(half) for half in join(from_x)]))
    kept = add_rows(kept, came)
    sums = kept[0].astype(f32)
    for apart in (1, 2, 3):
        sums = sums + seq_shift(kept[apart], apart).astype(f32)
    sums = sums.astype(bf16)
    others_crossed = [tuple(core_swap(half) for half in pair) for pair in others[:3]]
    early = early_product(lefts, mine, [own + crossed for own, crossed in zip(others, others_crossed)])
    early, last = lax.optimization_barrier((early, others[3]))
    product = late_product(y_at, lefts[1:], [*last, *[core_swap(half) for half in last]], early)

    strip, patch, cols = sums.shape[0] - samples, stud_head.shape[1], sums.shape[1]
    head_sums = sums[:strip, : 8 * patch].reshape(strip, 8, patch).transpose(1, 0, 2)
    d_mod = jnp.broadcast_to(sums[None, strip:], (8, samples, cols))
    emb = g_emb.reshape(samples, 8, freq // 8).transpose(1, 0, 2)
    sent = jnp.concatenate(
        [
            jnp.pad(head_sums, ((0, 0), (0, 0), (0, 128 - patch))),
            jnp.pad(d_mod, ((0, 0), (0, strip - samples), (0, 0))),
            jnp.pad(emb, ((0, 0), (0, strip - samples), (0, 128 - freq // 8))),
        ],
        axis=2,
    )
    got = lax.all_to_all(sent, "dp", 0, 0, tiled=True)
    grad_head = jnp.sum(got[:, :, :patch].astype(f32), axis=0)
    d_mods = got[:, :samples, 128 : 128 + cols].reshape(8 * samples, cols)
    embs = got[:, :samples, 128 + cols : 128 + cols + freq // 8].reshape(8 * samples, freq // 8)
    grad_guidance = dot_f32(embs, d_mods, 0, 0)

    total = product[0].astype(f32)
    for apart in (2, 1, 3):
        total = total + y_shift(product[apart], apart).astype(f32)
    grad_out_proj = total.T
    return (grad_out_proj, grad_head, grad_guidance)


def solution(mesh):
    placed = (
        P("pair", "dp", "seq", None),
        P("dp", ("seq", "pair"), None),
        P("dp", ("seq", "pair"), None),
        P("dp", ("seq", "pair"), None),
        P("dp", ("seq", "pair"), None),
        P("dp", None),
        P("dp", None),
        P("dp", None),
        P(None, ("seq", "pair")),
        P(None, ("seq", "pair")),
        P(),
        P(),
        P("seq", None),
    )
    return jax.shard_map(
        local,
        mesh=mesh,
        in_specs=placed,
        out_specs=(
            P("seq", ("dp", "pair")),
            P(("dp", "seq", "pair"), None),
            P("dp", ("seq", "pair")),
        ),
        check_vma=False,
    )
```

```python
import functools
import math

import jax
import jax.numpy as jnp
from jax import lax
from jax.experimental import pallas as pl
from jax.experimental.pallas import tpu as pltpu
from jax.sharding import PartitionSpec as P

HEAD_DIM = 128
VMEM_LIMIT = 56 * 1024 * 1024
FREE = pl.CostEstimate(flops=0, bytes_accessed=0, transcendentals=0)


def side(core):
    return 1 if core == 0 else -1


def seq_shift(value, apart):
    return lax.ppermute(value, "seq", [(i, ((i // 2 + apart) % 4) * 2 + i % 2) for i in range(8)])


def seq_ring(value):
    return lax.ppermute(value, "seq", [(i, ((i // 2 + side(i % 2)) % 4) * 2 + i % 2) for i in range(8)])


def core_swap(value):
    return lax.ppermute(value, "seq", [(i, i ^ 1) for i in range(8)])


def y_shift(value, apart):
    return lax.ppermute(value, "dp", [(i, ((i // 2 + apart) % 4) * 2 + i % 2) for i in range(8)])


def x_shift(value, apart):
    def target(index):
        data, seq, pair = index // 16, index // 2 % 8, index % 2
        x = (pair * 2 + data % 2 + side(seq % 2) * apart) % 4
        return (data // 2 * 2 + x % 2) * 16 + seq * 2 + x // 2

    return lax.ppermute(value, ("dp", "seq", "pair"), [(i, target(i)) for i in range(128)])


def pair_swap(value):
    return lax.ppermute(value, "pair", [(0, 1), (1, 0)])


def add_rows(left, right):
    return (left.astype(jnp.float32) + right.astype(jnp.float32)).astype(jnp.bfloat16)


def ring_reduce(low, high):
    totals = [seq_ring(low[0]), seq_ring(high[0])]
    for terms in zip(low[1:], high[1:]):
        totals = [seq_ring(add_rows(term, total)) for term, total in zip(terms, totals)]
    return totals


def ring_gather(block):
    blocks = [block]
    for _ in range(3):
        blocks.append(seq_ring(blocks[-1]))
    return blocks


def sinusoid(values, width):
    half = width // 2
    steps = jnp.arange(half, dtype=jnp.float32)
    freqs = jnp.exp(-math.log(10000.0) * steps / half)
    angles = values[..., None] * freqs
    return jnp.concatenate([jnp.cos(angles), jnp.sin(angles)], axis=-1)


def dot_f32(left, right, left_dim, right_dim):
    return lax.dot_general(
        left, right, (((left_dim,), (right_dim,)), ((), ())), preferred_element_type=jnp.float32
    )


def teacher_kernel(hidden_ref, hot_ref, table_ref, head_ref, out_ref):
    rows, width = hidden_ref.shape
    chunks = table_ref.shape[0] // 2
    cols = width // chunks
    hidden = hidden_ref[...].astype(jnp.float32)
    center = hidden - jnp.mean(hidden, axis=-1, keepdims=True)
    inverse = lax.rsqrt(jnp.mean(center * center, axis=-1, keepdims=True) + 1e-06)
    hot = hot_ref[...]
    total = jnp.zeros((rows, head_ref.shape[0]), jnp.float32)
    for i in range(chunks):
        part = slice(i * cols, (i + 1) * cols)
        shift = dot_f32(hot, table_ref[i], 1, 0)
        scale = dot_f32(hot, table_ref[chunks + i], 1, 0)
        normed = center[:, part] * inverse
        model_in = (normed * (1.0 + scale) + shift).astype(jnp.bfloat16)
        total += dot_f32(model_in, head_ref[:, part], 1, 1)
    out_ref[...] = total


def teacher(hidden, hot, table, head):
    rows, width = hidden.shape
    block = 128
    patch = head.shape[0]
    return pl.pallas_call(
        teacher_kernel,
        grid=(rows // block,),
        in_specs=[
            pl.BlockSpec((block, width), lambda i: (i, 0)),
            pl.BlockSpec((block, hot.shape[1]), lambda i: (i, 0)),
            pl.BlockSpec(table.shape, lambda i: (0, 0, 0)),
            pl.BlockSpec(head.shape, lambda i: (0, 0)),
        ],
        out_specs=pl.BlockSpec((block, patch), lambda i: (i, 0)),
        out_shape=jax.ShapeDtypeStruct((rows, patch), jnp.float32),
        compiler_params=pltpu.CompilerParams(vmem_limit_bytes=VMEM_LIMIT),
        cost_estimate=FREE,
        name="teacher",
    )(hidden, hot, table, head)


def pack_kernel(tensors, *refs):
    out_ref = refs[-1]
    groups = out_ref.shape[0]
    for g in range(groups):
        start = 0
        for ref in [refs[t * groups + g] for t in range(tensors)] + list(refs[tensors * groups : -1]):
            out_ref[g, start : start + ref.shape[0]] = ref[...]
            start += ref.shape[0]


def exchange(tensors, *shared):
    rows, width = tensors[0].shape
    groups, count = 8, len(tensors)
    cols = width // groups
    half = groups // 2
    height = count * rows + sum(array.shape[0] for array in shared)
    packed = pl.pallas_call(
        functools.partial(pack_kernel, count),
        grid=(2,),
        in_specs=[
            pl.BlockSpec((rows, cols), functools.partial(lambda g, i: (0, i * half + g), g))
            for _ in tensors
            for g in range(half)
        ]
        + [pl.BlockSpec(array.shape, lambda i: (0, 0)) for array in shared],
        out_specs=pl.BlockSpec((half, height, cols), lambda i: (i, 0, 0)),
        out_shape=jax.ShapeDtypeStruct((groups, height, cols), tensors[0].dtype),
        compiler_params=pltpu.CompilerParams(vmem_limit_bytes=VMEM_LIMIT),
        cost_estimate=FREE,
        name="pack",
    )(*[tensor for tensor in tensors for _ in range(half)], *shared)
    return lax.all_to_all(packed, "seq", 0, 0, tiled=True)


def rows_kernel(*refs):
    half = len(refs) // 2
    for source, out in zip(refs[:half], refs[half:]):
        out[...] = source[...]


def take_rows(pieces, *spans):
    blocks, _, cols = pieces.shape
    half = blocks // 2
    return pl.pallas_call(
        rows_kernel,
        grid=(2,),
        in_specs=[
            pl.BlockSpec((half, rows, cols), functools.partial(lambda at, i: (i, at, 0), start // rows))
            for start, rows in spans
        ],
        out_specs=[pl.BlockSpec((half, rows, cols), lambda i: (i, 0, 0)) for _, rows in spans],
        out_shape=[jax.ShapeDtypeStruct((blocks, rows, cols), pieces.dtype) for _, rows in spans],
        compiler_params=pltpu.CompilerParams(vmem_limit_bytes=16 * 1024 * 1024),
        cost_estimate=FREE,
        name="take_rows",
    )(*[pieces for _ in spans])


def attend_kernel(
    low_ref, high_ref, turn_ref, qseg_ref, kseg_ref, value_ref, first_ref, second_ref,
    out_ref, cross_ref, turned_ref, score_ref, top_ref, acc_ref,
):
    block = value_ref.shape[1]
    heads = value_ref.shape[2] // HEAD_DIM
    upper, lower = slice(0, block), slice(block, 2 * block)
    step = pl.program_id(0)
    low, high = low_ref[step], high_ref[step]
    factor = math.log2(math.e) / math.sqrt(HEAD_DIM)
    parts = [slice(h * HEAD_DIM, (h + 1) * HEAD_DIM) for h in range(heads)]
    top_ref[...] = jnp.full_like(top_ref, -1e30)
    acc_ref[...] = jnp.zeros_like(acc_ref)
    query_seg = qseg_ref[0]

    def score(index, carry):
        same = query_seg == kseg_ref[index]
        scores = [
            dot_f32(first_ref[turn_ref[step], lower, part], second_ref[index, :, part], 1, 1) for part in parts
        ]
        for h in range(heads):
            masked = jnp.where(same, scores[h] * factor, -1e30)
            score_ref[index - low, h] = masked
            pair = jnp.maximum(masked[:, :block], masked[:, block:])
            top_ref[h] = jnp.maximum(top_ref[h], pair)
        return carry

    lax.fori_loop(low, high, score, 0)
    for h in range(heads):
        top_ref[h] = jnp.broadcast_to(jnp.max(top_ref[h], axis=-1, keepdims=True), top_ref.shape[1:])
    ones = jnp.ones((2 * block, HEAD_DIM), jnp.bfloat16)

    def mix(index, carry):
        weights = []
        for h in range(heads):
            top = jnp.concatenate([top_ref[h], top_ref[h]], axis=1)
            weights.append(jnp.exp2(score_ref[index - low, h] - top).astype(jnp.bfloat16))
        for h, part in enumerate(parts):
            values = jnp.concatenate([first_ref[index, upper, part], value_ref[index, :, part]], axis=0)
            acc_ref[h] += dot_f32(weights[h], jnp.concatenate([values, ones], axis=1), 1, 0)
        return carry

    lax.fori_loop(low, high, mix, 0)
    result = jnp.concatenate(
        [acc_ref[h, :, :HEAD_DIM] / acc_ref[h, :, HEAD_DIM:] for h in range(heads)], axis=1
    )
    rounded = result.astype(jnp.bfloat16)

    @pl.when(step < 4)
    def _():
        out_ref[0] = rounded

    @pl.when(step >= 4)
    def _():
        cross_ref[0] = rounded

    turned = result.T.astype(jnp.bfloat16)
    arrival = lax.rem(8 - step, 4)
    for core in range(2):

        @pl.when(step // 4 == core)
        def _():
            turned_ref[arrival, :, core * block : (core + 1) * block] = turned


def attend(low, high, turn, query_seg, key_seg, value_other, first, second):
    blocks, block, width = value_other.shape
    chips = blocks // 2
    heads = width // HEAD_DIM

    def fixed(array):
        return pl.BlockSpec(array.shape, lambda j, *_: (0,) * array.ndim, pipeline_mode=pl.Buffered(1))

    return pl.pallas_call(
        attend_kernel,
        grid_spec=pltpu.PrefetchScalarGridSpec(
            num_scalar_prefetch=3,
            grid=(blocks,),
            in_specs=[pl.BlockSpec((1, block, 1), lambda j, *_: (j, 0, 0))]
            + [fixed(array) for array in (key_seg, value_other, first, second)],
            out_specs=[
                pl.BlockSpec((1, block, width), lambda j, *_: (jnp.minimum(j, 3), 0, 0)),
                pl.BlockSpec((1, block, width), lambda j, *_: (jnp.maximum(j - 4, 0), 0, 0)),
                pl.BlockSpec((chips, width, 2 * block), lambda j, *_: (0, 0, 0)),
            ],
            scratch_shapes=[
                pltpu.VMEM((6, heads, block, 2 * block), jnp.float32),
                pltpu.VMEM((heads, block, block), jnp.float32),
                pltpu.VMEM((heads, block, 2 * HEAD_DIM), jnp.float32),
            ],
        ),
        out_shape=[
            jax.ShapeDtypeStruct((chips, block, width), jnp.bfloat16),
            jax.ShapeDtypeStruct((chips, block, width), jnp.bfloat16),
            jax.ShapeDtypeStruct((chips, width, 2 * block), jnp.bfloat16),
        ],
        compiler_params=pltpu.CompilerParams(vmem_limit_bytes=24 * 1024 * 1024),
        cost_estimate=FREE,
        name="attend",
    )(low, high, turn, query_seg, key_seg, value_other, first, second)


def project_kernel(own_ref, crossed_ref, w_own_ref, w_crossed_ref, *refs):
    outs, left_ref = refs[:-1], refs[-1]
    chips, block, depth = own_ref.shape

    @pl.when(pl.program_id(0) == 0)
    def _():
        for k in range(chips):
            take, even = slice(k * block, (k + 1) * block), depth // 256 * 256
            left_ref[take, :even] = own_ref[k, :, :even]
            left_ref[take, even : 2 * even] = crossed_ref[k, :, :even]
            left_ref[take, 2 * even : depth + even] = own_ref[k, :, even:]
            left_ref[take, depth + even :] = crossed_ref[k, :, even:]

    even = depth // 256 * 256
    rest = jnp.concatenate([w_own_ref[even:, :], w_crossed_ref[even:, :]], axis=0)
    total = dot_f32(left_ref[:, :even], w_own_ref[:even, :], 1, 0)
    total += dot_f32(left_ref[:, even : 2 * even], w_crossed_ref[:even, :], 1, 0)
    total = (total + dot_f32(left_ref[:, 2 * even :], rest, 1, 0)).astype(jnp.bfloat16)
    start = 0
    for out in outs:
        out[...] = total[start : start + out.shape[0]]
        start += out.shape[0]


def project(own, crossed, w_own, w_crossed):
    chips, block, depth = own.shape
    width = w_own.shape[1]
    tile = 1024
    heights = [block] + [block // 2] * (2 * chips - 2)
    left = pl.BlockSpec(own.shape, lambda i: (0, 0, 0))
    right = pl.BlockSpec((depth, tile), lambda i: (0, i))
    return pl.pallas_call(
        project_kernel,
        grid=(width // tile,),
        in_specs=[left, left, right, right],
        out_specs=[pl.BlockSpec((height, tile), lambda i: (0, i)) for height in heights],
        out_shape=[jax.ShapeDtypeStruct((height, width), jnp.bfloat16) for height in heights],
        scratch_shapes=[pltpu.VMEM((chips * block, 2 * depth), jnp.bfloat16)],
        compiler_params=pltpu.CompilerParams(vmem_limit_bytes=VMEM_LIMIT),
        cost_estimate=FREE,
        name="project",
    )(own, crossed, w_own, w_crossed)


def join_kernel(*refs):
    half = refs[0].shape[0] // 2
    for k, ref in enumerate(refs[:-2]):
        refs[-2][k * half : (k + 1) * half, :] = ref[:half, :]
        refs[-1][k * half : (k + 1) * half, :] = ref[half:, :]


def join(pieces):
    rows, cols = pieces[0].shape
    out = jax.ShapeDtypeStruct((len(pieces) * rows // 2, cols), pieces[0].dtype)
    return pl.pallas_call(
        join_kernel,
        out_shape=[out, out],
        compiler_params=pltpu.CompilerParams(vmem_limit_bytes=16 * 1024 * 1024),
        cost_estimate=FREE,
        name="join",
    )(*pieces)


def student_kernel(
    x_ref, own_ref, la_ref, ha_ref, residual_ref, hot_ref, table_ref, head_ref, guided_ref,
    first_ref, second_ref, third_ref, fourth_ref, in_ref, kept_ref, resid_ref,
    stream_ref, normed_ref, dn_ref, dproj_ref,
):
    rows, width = residual_ref.shape
    chunks = table_ref.shape[0] // 2
    cols = width // chunks
    f32 = jnp.float32
    total = jnp.zeros((rows, 1), f32)
    for i in range(chunks):
        part = slice(i * cols, (i + 1) * cols)
        low, high = la_ref[:, part].astype(f32), ha_ref[:, part].astype(f32)
        base = residual_ref[:, part].astype(f32) + own_ref[:, part].astype(f32)
        stream = base + jnp.concatenate([low, high], axis=0)
        stream_ref[:, part] = stream
        total += jnp.sum(stream, axis=-1, keepdims=True)
    mean = total / width
    square = jnp.zeros((rows, 1), f32)
    for i in range(chunks):
        part = slice(i * cols, (i + 1) * cols)
        center = stream_ref[:, part] - mean
        square += jnp.sum(center * center, axis=-1, keepdims=True)
    inverse = lax.rsqrt(square / width + 1e-06)
    hot = hot_ref[...]
    velocity = jnp.zeros((rows, head_ref.shape[0]), f32)
    for i in range(chunks):
        part = slice(i * cols, (i + 1) * cols)
        normed = (stream_ref[:, part] - mean) * inverse
        shift = dot_f32(hot, table_ref[i], 1, 0)
        scale = 1.0 + dot_f32(hot, table_ref[chunks + i], 1, 0)
        model_in = (normed * scale + shift).astype(jnp.bfloat16)
        normed_ref[:, part] = normed
        kept_ref[:, part] = normed.astype(jnp.bfloat16)
        dn_ref[:, part] = scale
        in_ref[:, part] = model_in
        velocity += dot_f32(model_in, head_ref[:, part], 1, 1)
    scale_back = 1.0 / math.sqrt(16384)
    resid = ((velocity - guided_ref[...]) * scale_back).astype(jnp.bfloat16)
    resid_ref[...] = resid
    first = jnp.zeros((rows, 1), f32)
    second = jnp.zeros((rows, 1), f32)
    for i in range(chunks):
        part = slice(i * cols, (i + 1) * cols)
        cotangent = dot_f32(resid, head_ref[:, part], 1, 0)
        normed = normed_ref[:, part]
        dnorm = cotangent * dn_ref[:, part]
        dn_ref[:, part] = dnorm
        first += jnp.sum(dnorm, axis=-1, keepdims=True)
        second += jnp.sum(dnorm * normed, axis=-1, keepdims=True)
    first = first / width
    second = second / width

    def back(chunk):
        part = slice(chunk * cols, (chunk + 1) * cols)
        return inverse * (dn_ref[:, part] - first - normed_ref[:, part] * second)

    side = cols // 2
    for lo in range(2):
        for y in range(0, 4, 2):
            even, odd = back(2 * y + lo), back(2 * y + 2 + lo)
            for hi in range(2):
                cut = slice(hi * side, (hi + 1) * side)
                both = jnp.concatenate([even[:, cut], odd[:, cut]], axis=1)
                dproj_ref[hi * 2 + lo, :, (y // 2) * cols : (y // 2 + 1) * cols] = both.astype(jnp.bfloat16)
    for apart, ref in enumerate((first_ref, second_ref, third_ref, fourth_ref)):
        ref[...] = dproj_ref[lax.rem(x_ref[0] + 4 + x_ref[1] * apart, 4)]

def student(chip_x, own, received, residual, hot, table, head, guided):
    rows, width = residual.shape
    quarter = width // 4
    arrays = (own, *received, residual, hot, table, head, guided)
    outs = [(rows, quarter)] * 4 + [(rows, width), (rows, width), guided.shape]
    return pl.pallas_call(
        student_kernel,
        grid_spec=pltpu.PrefetchScalarGridSpec(
            num_scalar_prefetch=1,
            grid=(1,),
            in_specs=[
                pl.BlockSpec(array.shape, functools.partial(lambda dims, i, p: (0,) * dims, array.ndim))
                for array in arrays
            ],
            out_specs=[pl.BlockSpec(out, lambda i, p: (0, 0)) for out in outs],
            scratch_shapes=[
                pltpu.VMEM((rows, width), jnp.float32),
                pltpu.VMEM((rows, width), jnp.float32),
                pltpu.VMEM((rows, width), jnp.float32),
                pltpu.VMEM((4, rows, quarter), jnp.bfloat16),
            ],
        ),
        out_shape=[jax.ShapeDtypeStruct(out, jnp.bfloat16) for out in outs],
        compiler_params=pltpu.CompilerParams(vmem_limit_bytes=40 * 1024 * 1024),
        cost_estimate=FREE,
        name="student",
    )(chip_x, *arrays)


def sums_kernel(
    place_ref, in_ref, normed_ref, resid_ref, hot_ref, head_ref, own_ref, cross_ref, headpart_ref, mod_ref, out_ref
):
    f32, bf16 = jnp.float32, jnp.bfloat16
    chunks, cols, patch = headpart_ref.shape
    samples = mod_ref.shape[1]
    resid = resid_ref[...]
    hot = hot_ref[:, hot_ref.shape[1] - samples :]
    for i in range(chunks):
        part = slice(i * cols, (i + 1) * cols)
        cotangent = dot_f32(resid, head_ref[:, part], 1, 0)
        headpart_ref[i] = dot_f32(in_ref[:, part], resid, 0, 0)
        mod_ref[i] = dot_f32(hot, cotangent.astype(bf16), 0, 0)
        scaled = cotangent * normed_ref[:, part].astype(f32)
        mod_ref[chunks + i] = dot_f32(hot, scaled.astype(bf16), 0, 0)
    strip = cols // (2 * chunks)
    blank = jnp.zeros((strip, cols - chunks * patch), f32)
    for i in range(2 * chunks):
        take = slice(i * strip, (i + 1) * strip)
        head_rows = jnp.concatenate([headpart_ref[k, take, :] for k in range(chunks)] + [blank], axis=1)
        out_ref[i] = jnp.concatenate([head_rows, mod_ref[i]], axis=0).astype(bf16)
    for core, ref in enumerate((own_ref, cross_ref)):
        for pair in range(2):
            for chip in range(4):
                z, c, p = lax.rem(place_ref[0] + chip, 4), lax.rem(place_ref[1] + core, 2), lax.rem(place_ref[2] + pair, 2)
                ref[pair, chip] = out_ref[z * 4 + c * 2 + p]


def local_sums(place, model_in, normed, resid, hot, head, samples, devices):
    rows, width = model_in.shape
    chunk = 2 * width // devices
    part = (chunk // devices + samples, chunk)
    arrays = (model_in, normed, resid, hot, head)
    out = (2, devices // 4) + part
    return pl.pallas_call(
        sums_kernel,
        grid_spec=pltpu.PrefetchScalarGridSpec(
            num_scalar_prefetch=1,
            grid=(1,),
            in_specs=[pl.BlockSpec(array.shape, lambda i, p: (0, 0)) for array in arrays],
            out_specs=[pl.BlockSpec(out, lambda i, p: (0, 0, 0, 0)) for _ in range(2)],
            scratch_shapes=[
                pltpu.VMEM((devices // 2, chunk, head.shape[0]), jnp.float32),
                pltpu.VMEM((devices, samples, chunk), jnp.float32),
                pltpu.VMEM((devices,) + part, jnp.bfloat16),
            ],
        ),
        out_shape=[jax.ShapeDtypeStruct(out, jnp.bfloat16) for _ in range(2)],
        compiler_params=pltpu.CompilerParams(vmem_limit_bytes=24 * 1024 * 1024),
        cost_estimate=FREE,
        name="local_sums",
    )(place, *arrays)


def block_rows(refs, position):
    half = 64
    places = (position, position, 2 - position, 2 - position)
    return jnp.concatenate([ref[at * half : (at + 1) * half, :] for ref, at in zip(refs, places)], axis=0)


def early_kernel(*refs):
    out_ref, lefts, refs = refs[-1], refs[:4], refs[4:-1]
    total = jnp.zeros(out_ref.shape, jnp.float32)
    for arrival in range(4):
        rows = jnp.concatenate([refs[0][...], refs[1][...]], axis=0)
        total += dot_f32(lefts[0][arrival], rows, 1, 0)
        refs = refs[2:]
    for arrival in range(3):
        for position in range(3):
            total += dot_f32(lefts[1 + position][arrival], block_rows(refs[:4], position), 1, 0)
        refs = refs[4:]
    out_ref[...] = total


def early_product(lefts, mine, others):
    tile = 256
    flat = [part for blocks in (mine, others) for parts in blocks for part in parts]
    depth, width = lefts[0].shape[1], flat[0].shape[1]
    return pl.pallas_call(
        early_kernel,
        grid=(width // tile,),
        in_specs=[pl.BlockSpec(left.shape, lambda i: (0, 0, 0)) for left in lefts]
        + [pl.BlockSpec((part.shape[0], tile), lambda i: (0, i)) for part in flat],
        out_specs=pl.BlockSpec((depth, tile), lambda i: (0, i)),
        out_shape=jax.ShapeDtypeStruct((depth, width), jnp.float32),
        compiler_params=pltpu.CompilerParams(vmem_limit_bytes=50 * 1024 * 1024),
        cost_estimate=FREE,
        name="early_product",
    )(*lefts, *flat)


def late_kernel(y_ref, first_ref, second_ref, third_ref, a_ref, b_ref, c_ref, d_ref, early_ref, *refs):
    outs, turned_ref = refs[:-1], refs[-1]
    step = pl.program_id(0)
    tile = early_ref.shape[1]
    total = early_ref[...]
    for position, left in enumerate((first_ref, second_ref, third_ref)):
        total += dot_f32(left[0], block_rows((a_ref, b_ref, c_ref, d_ref), position), 1, 0)
    turned_ref[pl.ds(pl.multiple_of(step * tile, tile), tile), :] = total.T.astype(jnp.bfloat16)

    @pl.when(step == pl.num_programs(0) - 1)
    def _():
        rows = outs[0].shape[0]
        for apart, out in enumerate(outs):
            start = pl.multiple_of(lax.rem(y_ref[0] + apart, 4) * rows, rows)
            out[...] = turned_ref[pl.ds(start, rows), :]


def late_product(chip_y, lefts, flat, early):
    depth, width = early.shape
    tile = 256
    return pl.pallas_call(
        late_kernel,
        grid_spec=pltpu.PrefetchScalarGridSpec(
            num_scalar_prefetch=1,
            grid=(width // tile,),
            in_specs=[pl.BlockSpec((1,) + left.shape[1:], lambda i, p: (3, 0, 0)) for left in lefts]
            + [pl.BlockSpec((half.shape[0], tile), lambda i, p: (0, i)) for half in flat]
            + [pl.BlockSpec((depth, tile), lambda i, p: (0, i))],
            out_specs=[pl.BlockSpec((width // 4, depth), lambda i, p: (0, 0)) for _ in range(4)],
            scratch_shapes=[pltpu.VMEM((width, depth), jnp.bfloat16)],
        ),
        out_shape=[jax.ShapeDtypeStruct((width // 4, depth), jnp.bfloat16) for _ in range(4)],
        compiler_params=pltpu.CompilerParams(vmem_limit_bytes=VMEM_LIMIT),
        cost_estimate=FREE,
        name="late_product",
    )(chip_y, *lefts, *flat, early)


def local(
    teacher_hidden,
    student_query,
    student_key,
    student_value,
    residual,
    segment_ids,
    timesteps,
    guide_scales,
    time_proj,
    guide_proj,
    teach_head,
    stud_head,
    out_proj,
):
    bf16, f32 = jnp.bfloat16, jnp.float32
    seq_pos, pair_pos, data_pos = lax.axis_index("seq"), lax.axis_index("pair"), lax.axis_index("dp")
    chip_z, core = seq_pos // 2, seq_pos % 2
    chip_y, chip_x = data_pos // 2, pair_pos * 2 + data_pos % 2
    segment = segment_ids[0]
    samples = timesteps.shape[1]
    freq = time_proj.shape[0]

    guidance = guide_scales[0].astype(f32) / 8.0
    t_emb = sinusoid(timesteps[0].astype(f32), freq).astype(bf16)
    g_emb = sinusoid(1000.0 * guidance, freq).astype(bf16)
    teach_cols = jnp.dot(t_emb, time_proj, preferred_element_type=f32)
    stud_cols = teach_cols + jnp.dot(g_emb, guide_proj, preferred_element_type=f32)
    columns = jnp.concatenate([teach_cols, stud_cols], axis=0).astype(bf16)

    stud_rows = student_query.shape[1]
    ids = jnp.arange(2 * samples, dtype=jnp.int32)[None, :]
    hidden = teacher_hidden[0, 0]
    teach_seg = lax.dynamic_slice_in_dim(segment, seq_pos * hidden.shape[0], hidden.shape[0])
    stud_seg = lax.dynamic_slice_in_dim(teach_seg, pair_pos * stud_rows, stud_rows)
    teach_hot = (teach_seg[:, None] == ids).astype(bf16)
    stud_hot = (stud_seg[:, None] == ids - samples).astype(bf16)
    guide_tok = jnp.sum(
        jnp.where(stud_seg[:, None] == ids[:, :samples], guidance[None, :], 0.0), axis=1, keepdims=True
    )

    by_block = segment.reshape(8, 2, stud_rows)
    own_seg = lax.dynamic_index_in_dim(by_block, pair_pos, 1, keepdims=False)
    other_seg = lax.dynamic_index_in_dim(by_block, 1 - pair_pos, 1, keepdims=False)
    turn = jnp.arange(8, dtype=jnp.int32)
    away = ((1 - 2 * core) * (1 - 2 * (turn // 4)) * (turn % 4) + 4) % 4
    spots = (chip_z + away) % 4 * 2 + (core + turn // 4) % 2
    query_seg = own_seg[spots]
    low = jnp.sum((segment[None, :] < query_seg[:, :1]).astype(jnp.int32), axis=1) // 256
    high = (jnp.sum((segment[None, :] <= query_seg[:, -1:]).astype(jnp.int32), axis=1) + 255) // 256
    segs = query_seg[:, :, None], jnp.concatenate([own_seg, other_seg], axis=1)[:, None, :]

    key_crossed, weights_crossed = pair_swap(student_key[0]), core_swap(out_proj)
    first = exchange([student_value[0], student_query[0]], columns)
    first, key_crossed = lax.optimization_barrier((first, key_crossed))
    value_own, table = take_rows(first, (0, stud_rows), (2 * stud_rows, columns.shape[0]))
    value_own, table_other = lax.optimization_barrier((value_own, pair_swap(table)))
    value_other = pair_swap(value_own)
    second = exchange([student_key[0], key_crossed])
    lower, upper = jnp.where(pair_pos == 0, table, table_other), jnp.where(pair_pos == 0, table_other, table)
    table = jnp.stack([lower, upper], axis=1).reshape((16,) + columns.shape)
    velocity = teacher(hidden, teach_hot, table, teach_head.T)
    own_vel = lax.dynamic_slice_in_dim(velocity, pair_pos * stud_rows, stud_rows, 0)
    sent_vel = lax.dynamic_slice_in_dim(velocity, (1 - pair_pos) * stud_rows, stud_rows, 0)
    value_other, second, weights_crossed, low, high, segs, sent_vel = lax.optimization_barrier(
        (value_other, second, weights_crossed, low, high, segs, sent_vel)
    )
    attn_own, attn_cross, turned = attend(
        low, high, spots, *segs, value_other, first, second
    )

    own, *terms = project(attn_own, core_swap(attn_cross), out_proj, weights_crossed)
    received = ring_reduce(terms[4::-2], terms[5::-2])
    lefts = [turned]
    for _ in range(2):
        lefts.append(x_shift(lefts[-1], 1))
    other_vel = pair_swap(sent_vel.astype(bf16)).astype(f32)
    cond_vel = jnp.where(pair_pos == 0, own_vel, other_vel)
    uncond_vel = jnp.where(pair_pos == 0, other_vel, own_vel)
    guided = uncond_vel + guide_tok * (cond_vel - uncond_vel)
    own, lefts[1:3], guided = lax.optimization_barrier((own, lefts[1:3], guided))

    x_at = jnp.stack([chip_x, 1 - 2 * core]).astype(jnp.int32)
    y_at = jnp.reshape(chip_y, (1,)).astype(jnp.int32)
    *quarters, model_in, normed, resid = student(
        x_at, own, received, residual[0], stud_hot, table, stud_head.T, guided
    )

    from_x = [x_shift(quarters[apart], apart) for apart in (1, 2, 3)]
    mine = [quarters[0], seq_ring(quarters[0])]
    at = jnp.stack([chip_z, core, pair_pos]).astype(jnp.int32)
    kept, sent = local_sums(at, model_in, normed, resid, stud_hot, stud_head.T, samples, table.shape[0])
    from_x, kept, sent, mine[1] = lax.optimization_barrier((from_x, kept, sent, mine[1]))
    for _ in range(2):
        mine.append(seq_ring(mine[-1]))
    mine = [(block, core_swap(block)) for block in mine]
    came = core_swap(sent)
    kept, sent = add_rows(kept[0], came[0]), add_rows(kept[1], came[1])
    came = pair_swap(sent)
    came, lefts[2] = lax.optimization_barrier((came, lefts[2]))
    lefts.append(x_shift(lefts[2], 1))
    others = list(zip(*[ring_gather(half) for half in join(from_x)]))
    kept = add_rows(kept, came)
    sums = kept[0].astype(f32)
    for apart in (1, 2, 3):
        sums = sums + seq_shift(kept[apart], apart).astype(f32)
    sums = sums.astype(bf16)
    others_crossed = [tuple(core_swap(half) for half in pair) for pair in others[:3]]
    early = early_product(lefts, mine, [own + crossed for own, crossed in zip(others, others_crossed)])
    early, last = lax.optimization_barrier((early, others[3]))
    product = late_product(y_at, lefts[1:], [*last, *[core_swap(half) for half in last]], early)

    strip, patch, cols = sums.shape[0] - samples, stud_head.shape[1], sums.shape[1]
    head_sums = sums[:strip, : 8 * patch].reshape(strip, 8, patch).transpose(1, 0, 2)
    d_mod = jnp.broadcast_to(sums[None, strip:], (8, samples, cols))
    emb = g_emb.reshape(samples, 8, freq // 8).transpose(1, 0, 2)
    sent = jnp.concatenate(
        [
            jnp.pad(head_sums, ((0, 0), (0, 0), (0, 128 - patch))),
            jnp.pad(d_mod, ((0, 0), (0, strip - samples), (0, 0))),
            jnp.pad(emb, ((0, 0), (0, strip - samples), (0, 128 - freq // 8))),
        ],
        axis=2,
    )
    got = lax.all_to_all(sent, "dp", 0, 0, tiled=True)
    grad_head = jnp.sum(got[:, :, :patch].astype(f32), axis=0)
    d_mods = got[:, :samples, 128 : 128 + cols].reshape(8 * samples, cols)
    embs = got[:, :samples, 128 + cols : 128 + cols + freq // 8].reshape(8 * samples, freq // 8)
    grad_guidance = dot_f32(embs, d_mods, 0, 0)

    total = product[0].astype(f32)
    for apart in (2, 1, 3):
        total = total + y_shift(product[apart], apart).astype(f32)
    grad_out_proj = total.T
    return (grad_out_proj, grad_head, grad_guidance)


def solution(mesh):
    placed = (
        P("pair", "dp", "seq", None),
        P("dp", ("seq", "pair"), None),
        P("dp", ("seq", "pair"), None),
        P("dp", ("seq", "pair"), None),
        P("dp", ("seq", "pair"), None),
        P("dp", None),
        P("dp", None),
        P("dp", None),
        P(None, ("seq", "pair")),
        P(None, ("seq", "pair")),
        P(),
        P(),
        P("seq", None),
    )
    return jax.shard_map(
        local,
        mesh=mesh,
        in_specs=placed,
        out_specs=(
            P("seq", ("dp", "pair")),
            P(("dp", "seq", "pair"), None),
            P("dp", ("seq", "pair")),
        ),
        check_vma=False,
    )
```

```python
import functools
import math

import jax
import jax.numpy as jnp
from jax import lax
from jax.experimental import pallas as pl
from jax.experimental.pallas import tpu as pltpu
from jax.sharding import PartitionSpec as P

HEAD_DIM = 128
VMEM_LIMIT = 56 * 1024 * 1024
FREE = pl.CostEstimate(flops=0, bytes_accessed=0, transcendentals=0)


def side(core):
    return 1 if core == 0 else -1


def seq_shift(value, apart):
    return lax.ppermute(value, "seq", [(i, ((i // 2 + apart) % 4) * 2 + i % 2) for i in range(8)])


def seq_ring(value):
    return lax.ppermute(value, "seq", [(i, ((i // 2 + side(i % 2)) % 4) * 2 + i % 2) for i in range(8)])


def core_swap(value):
    return lax.ppermute(value, "seq", [(i, i ^ 1) for i in range(8)])


def y_shift(value, apart):
    return lax.ppermute(value, "dp", [(i, ((i // 2 + apart) % 4) * 2 + i % 2) for i in range(8)])


def x_shift(value, apart):
    def target(index):
        data, seq, pair = index // 16, index // 2 % 8, index % 2
        x = (pair * 2 + data % 2 + side(seq % 2) * apart) % 4
        return (data // 2 * 2 + x % 2) * 16 + seq * 2 + x // 2

    return lax.ppermute(value, ("dp", "seq", "pair"), [(i, target(i)) for i in range(128)])


def pair_swap(value):
    return lax.ppermute(value, "pair", [(0, 1), (1, 0)])


def add_rows(left, right):
    return (left.astype(jnp.float32) + right.astype(jnp.float32)).astype(jnp.bfloat16)


def ring_reduce(low, high):
    totals = [seq_ring(low[0]), seq_ring(high[0])]
    for terms in zip(low[1:], high[1:]):
        totals = [seq_ring(add_rows(term, total)) for term, total in zip(terms, totals)]
    return totals


def ring_gather(block):
    blocks = [block]
    for _ in range(3):
        blocks.append(seq_ring(blocks[-1]))
    return blocks


def sinusoid(values, width):
    half = width // 2
    steps = jnp.arange(half, dtype=jnp.float32)
    freqs = jnp.exp(-math.log(10000.0) * steps / half)
    angles = values[..., None] * freqs
    return jnp.concatenate([jnp.cos(angles), jnp.sin(angles)], axis=-1)


def dot_f32(left, right, left_dim, right_dim):
    return lax.dot_general(
        left, right, (((left_dim,), (right_dim,)), ((), ())), preferred_element_type=jnp.float32
    )


def teacher_kernel(hidden_ref, hot_ref, table_ref, head_ref, out_ref):
    rows, width = hidden_ref.shape
    chunks = table_ref.shape[0] // 2
    cols = width // chunks
    hidden = hidden_ref[...].astype(jnp.float32)
    center = hidden - jnp.mean(hidden, axis=-1, keepdims=True)
    inverse = lax.rsqrt(jnp.mean(center * center, axis=-1, keepdims=True) + 1e-06)
    hot = hot_ref[...]
    total = jnp.zeros((rows, head_ref.shape[0]), jnp.float32)
    for i in range(chunks):
        part = slice(i * cols, (i + 1) * cols)
        shift = dot_f32(hot, table_ref[i], 1, 0)
        scale = dot_f32(hot, table_ref[chunks + i], 1, 0)
        normed = center[:, part] * inverse
        model_in = (normed * (1.0 + scale) + shift).astype(jnp.bfloat16)
        total += dot_f32(model_in, head_ref[:, part], 1, 1)
    out_ref[...] = total


def teacher(hidden, hot, table, head):
    rows, width = hidden.shape
    block = 128
    patch = head.shape[0]
    return pl.pallas_call(
        teacher_kernel,
        grid=(rows // block,),
        in_specs=[
            pl.BlockSpec((block, width), lambda i: (i, 0)),
            pl.BlockSpec((block, hot.shape[1]), lambda i: (i, 0)),
            pl.BlockSpec(table.shape, lambda i: (0, 0, 0)),
            pl.BlockSpec(head.shape, lambda i: (0, 0)),
        ],
        out_specs=pl.BlockSpec((block, patch), lambda i: (i, 0)),
        out_shape=jax.ShapeDtypeStruct((rows, patch), jnp.float32),
        compiler_params=pltpu.CompilerParams(vmem_limit_bytes=VMEM_LIMIT),
        cost_estimate=FREE,
        name="teacher",
    )(hidden, hot, table, head)


def pack_kernel(tensors, *refs):
    out_ref = refs[-1]
    groups = out_ref.shape[0]
    for g in range(groups):
        start = 0
        for ref in [refs[t * groups + g] for t in range(tensors)] + list(refs[tensors * groups : -1]):
            out_ref[g, start : start + ref.shape[0]] = ref[...]
            start += ref.shape[0]


def exchange(tensors, *shared):
    rows, width = tensors[0].shape
    groups, count = 8, len(tensors)
    cols = width // groups
    half = groups // 2
    height = count * rows + sum(array.shape[0] for array in shared)
    packed = pl.pallas_call(
        functools.partial(pack_kernel, count),
        grid=(2,),
        in_specs=[
            pl.BlockSpec((rows, cols), functools.partial(lambda g, i: (0, i * half + g), g))
            for _ in tensors
            for g in range(half)
        ]
        + [pl.BlockSpec(array.shape, lambda i: (0, 0)) for array in shared],
        out_specs=pl.BlockSpec((half, height, cols), lambda i: (i, 0, 0)),
        out_shape=jax.ShapeDtypeStruct((groups, height, cols), tensors[0].dtype),
        compiler_params=pltpu.CompilerParams(vmem_limit_bytes=24 * 1024 * 1024),
        cost_estimate=FREE,
        name="pack",
    )(*[tensor for tensor in tensors for _ in range(half)], *shared)
    return lax.all_to_all(packed, "seq", 0, 0, tiled=True)


def rows_kernel(*refs):
    half = len(refs) // 2
    for source, out in zip(refs[:half], refs[half:]):
        out[...] = source[...]


def take_rows(pieces, *spans):
    blocks, _, cols = pieces.shape
    half = blocks // 2
    return pl.pallas_call(
        rows_kernel,
        grid=(2,),
        in_specs=[
            pl.BlockSpec((half, rows, cols), functools.partial(lambda at, i: (i, at, 0), start // rows))
            for start, rows in spans
        ],
        out_specs=[pl.BlockSpec((half, rows, cols), lambda i: (i, 0, 0)) for _, rows in spans],
        out_shape=[jax.ShapeDtypeStruct((blocks, rows, cols), pieces.dtype) for _, rows in spans],
        compiler_params=pltpu.CompilerParams(vmem_limit_bytes=16 * 1024 * 1024),
        cost_estimate=FREE,
        name="take_rows",
    )(*[pieces for _ in spans])


def attend_kernel(
    low_ref, high_ref, turn_ref, qseg_ref, kseg_ref, value_ref, first_ref, second_ref,
    out_ref, cross_ref, turned_ref, score_ref, top_ref, acc_ref,
):
    block = value_ref.shape[1]
    heads = value_ref.shape[2] // HEAD_DIM
    upper, lower = slice(0, block), slice(block, 2 * block)
    step = pl.program_id(0)
    low, high = low_ref[step], high_ref[step]
    factor = math.log2(math.e) / math.sqrt(HEAD_DIM)
    parts = [slice(h * HEAD_DIM, (h + 1) * HEAD_DIM) for h in range(heads)]
    top_ref[...] = jnp.full_like(top_ref, -1e30)
    acc_ref[...] = jnp.zeros_like(acc_ref)
    query_seg = qseg_ref[0]

    def score(index, carry):
        same = query_seg == kseg_ref[index]
        scores = [
            dot_f32(first_ref[turn_ref[step], lower, part], second_ref[index, :, part], 1, 1) for part in parts
        ]
        for h in range(heads):
            masked = jnp.where(same, scores[h] * factor, -1e30)
            score_ref[index - low, h] = masked
            pair = jnp.maximum(masked[:, :block], masked[:, block:])
            top_ref[h] = jnp.maximum(top_ref[h], pair)
        return carry

    lax.fori_loop(low, high, score, 0)
    for h in range(heads):
        top_ref[h] = jnp.broadcast_to(jnp.max(top_ref[h], axis=-1, keepdims=True), top_ref.shape[1:])
    ones = jnp.ones((2 * block, HEAD_DIM), jnp.bfloat16)

    def mix(index, carry):
        weights = []
        for h in range(heads):
            top = jnp.concatenate([top_ref[h], top_ref[h]], axis=1)
            weights.append(jnp.exp2(score_ref[index - low, h] - top).astype(jnp.bfloat16))
        for h, part in enumerate(parts):
            values = jnp.concatenate([first_ref[index, upper, part], value_ref[index, :, part]], axis=0)
            acc_ref[h] += dot_f32(weights[h], jnp.concatenate([values, ones], axis=1), 1, 0)
        return carry

    lax.fori_loop(low, high, mix, 0)
    result = jnp.concatenate(
        [acc_ref[h, :, :HEAD_DIM] / acc_ref[h, :, HEAD_DIM:] for h in range(heads)], axis=1
    )
    rounded = result.astype(jnp.bfloat16)

    @pl.when(step < 4)
    def _():
        out_ref[0] = rounded

    @pl.when(step >= 4)
    def _():
        cross_ref[0] = rounded

    turned = result.T.astype(jnp.bfloat16)
    arrival = lax.rem(8 - step, 4)
    for core in range(2):

        @pl.when(step // 4 == core)
        def _():
            turned_ref[arrival, :, core * block : (core + 1) * block] = turned


def attend(low, high, turn, query_seg, key_seg, value_other, first, second):
    blocks, block, width = value_other.shape
    chips = blocks // 2
    heads = width // HEAD_DIM

    def fixed(array):
        return pl.BlockSpec(array.shape, lambda j, *_: (0,) * array.ndim, pipeline_mode=pl.Buffered(1))

    return pl.pallas_call(
        attend_kernel,
        grid_spec=pltpu.PrefetchScalarGridSpec(
            num_scalar_prefetch=3,
            grid=(blocks,),
            in_specs=[pl.BlockSpec((1, block, 1), lambda j, *_: (j, 0, 0))]
            + [fixed(array) for array in (key_seg, value_other, first, second)],
            out_specs=[
                pl.BlockSpec((1, block, width), lambda j, *_: (jnp.minimum(j, 3), 0, 0)),
                pl.BlockSpec((1, block, width), lambda j, *_: (jnp.maximum(j - 4, 0), 0, 0)),
                pl.BlockSpec((chips, width, 2 * block), lambda j, *_: (0, 0, 0)),
            ],
            scratch_shapes=[
                pltpu.VMEM((6, heads, block, 2 * block), jnp.float32),
                pltpu.VMEM((heads, block, block), jnp.float32),
                pltpu.VMEM((heads, block, 2 * HEAD_DIM), jnp.float32),
            ],
        ),
        out_shape=[
            jax.ShapeDtypeStruct((chips, block, width), jnp.bfloat16),
            jax.ShapeDtypeStruct((chips, block, width), jnp.bfloat16),
            jax.ShapeDtypeStruct((chips, width, 2 * block), jnp.bfloat16),
        ],
        compiler_params=pltpu.CompilerParams(vmem_limit_bytes=24 * 1024 * 1024),
        cost_estimate=FREE,
        name="attend",
    )(low, high, turn, query_seg, key_seg, value_other, first, second)


def project_kernel(own_ref, crossed_ref, w_own_ref, w_crossed_ref, *refs):
    outs, left_ref = refs[:-1], refs[-1]
    chips, block, depth = own_ref.shape

    @pl.when(pl.program_id(0) == 0)
    def _():
        for k in range(chips):
            take, even = slice(k * block, (k + 1) * block), depth // 256 * 256
            left_ref[take, :even] = own_ref[k, :, :even]
            left_ref[take, even : 2 * even] = crossed_ref[k, :, :even]
            left_ref[take, 2 * even : depth + even] = own_ref[k, :, even:]
            left_ref[take, depth + even :] = crossed_ref[k, :, even:]

    even = depth // 256 * 256
    rest = jnp.concatenate([w_own_ref[even:, :], w_crossed_ref[even:, :]], axis=0)
    total = dot_f32(left_ref[:, :even], w_own_ref[:even, :], 1, 0)
    total += dot_f32(left_ref[:, even : 2 * even], w_crossed_ref[:even, :], 1, 0)
    total = (total + dot_f32(left_ref[:, 2 * even :], rest, 1, 0)).astype(jnp.bfloat16)
    start = 0
    for out in outs:
        out[...] = total[start : start + out.shape[0]]
        start += out.shape[0]


def project(own, crossed, w_own, w_crossed):
    chips, block, depth = own.shape
    width = w_own.shape[1]
    tile = 1024
    heights = [block] + [block // 2] * (2 * chips - 2)
    left = pl.BlockSpec(own.shape, lambda i: (0, 0, 0))
    right = pl.BlockSpec((depth, tile), lambda i: (0, i))
    return pl.pallas_call(
        project_kernel,
        grid=(width // tile,),
        in_specs=[left, left, right, right],
        out_specs=[pl.BlockSpec((height, tile), lambda i: (0, i)) for height in heights],
        out_shape=[jax.ShapeDtypeStruct((height, width), jnp.bfloat16) for height in heights],
        scratch_shapes=[pltpu.VMEM((chips * block, 2 * depth), jnp.bfloat16)],
        compiler_params=pltpu.CompilerParams(vmem_limit_bytes=VMEM_LIMIT),
        cost_estimate=FREE,
        name="project",
    )(own, crossed, w_own, w_crossed)


def join_kernel(*refs):
    half = refs[0].shape[0] // 2
    for k, ref in enumerate(refs[:-2]):
        refs[-2][k * half : (k + 1) * half, :] = ref[:half, :]
        refs[-1][k * half : (k + 1) * half, :] = ref[half:, :]


def join(pieces):
    rows, cols = pieces[0].shape
    out = jax.ShapeDtypeStruct((len(pieces) * rows // 2, cols), pieces[0].dtype)
    return pl.pallas_call(
        join_kernel,
        out_shape=[out, out],
        compiler_params=pltpu.CompilerParams(vmem_limit_bytes=16 * 1024 * 1024),
        cost_estimate=FREE,
        name="join",
    )(*pieces)


def student_kernel(
    x_ref, own_ref, la_ref, ha_ref, residual_ref, hot_ref, table_ref, head_ref, guided_ref,
    first_ref, second_ref, third_ref, fourth_ref, in_ref, kept_ref, resid_ref,
    stream_ref, normed_ref, dn_ref, dproj_ref,
):
    rows, width = residual_ref.shape
    chunks = table_ref.shape[0] // 2
    cols = width // chunks
    f32 = jnp.float32
    total = jnp.zeros((rows, 1), f32)
    for i in range(chunks):
        part = slice(i * cols, (i + 1) * cols)
        low, high = la_ref[:, part].astype(f32), ha_ref[:, part].astype(f32)
        base = residual_ref[:, part].astype(f32) + own_ref[:, part].astype(f32)
        stream = base + jnp.concatenate([low, high], axis=0)
        stream_ref[:, part] = stream
        total += jnp.sum(stream, axis=-1, keepdims=True)
    mean = total / width
    square = jnp.zeros((rows, 1), f32)
    for i in range(chunks):
        part = slice(i * cols, (i + 1) * cols)
        center = stream_ref[:, part] - mean
        square += jnp.sum(center * center, axis=-1, keepdims=True)
    inverse = lax.rsqrt(square / width + 1e-06)
    hot = hot_ref[...]
    velocity = jnp.zeros((rows, head_ref.shape[0]), f32)
    for i in range(chunks):
        part = slice(i * cols, (i + 1) * cols)
        normed = (stream_ref[:, part] - mean) * inverse
        shift = dot_f32(hot, table_ref[i], 1, 0)
        scale = 1.0 + dot_f32(hot, table_ref[chunks + i], 1, 0)
        model_in = (normed * scale + shift).astype(jnp.bfloat16)
        normed_ref[:, part] = normed
        kept_ref[:, part] = normed.astype(jnp.bfloat16)
        dn_ref[:, part] = scale
        in_ref[:, part] = model_in
        velocity += dot_f32(model_in, head_ref[:, part], 1, 1)
    scale_back = 1.0 / math.sqrt(16384)
    resid = ((velocity - guided_ref[...]) * scale_back).astype(jnp.bfloat16)
    resid_ref[...] = resid
    first = jnp.zeros((rows, 1), f32)
    second = jnp.zeros((rows, 1), f32)
    for i in range(chunks):
        part = slice(i * cols, (i + 1) * cols)
        cotangent = dot_f32(resid, head_ref[:, part], 1, 0)
        normed = normed_ref[:, part]
        dnorm = cotangent * dn_ref[:, part]
        dn_ref[:, part] = dnorm
        first += jnp.sum(dnorm, axis=-1, keepdims=True)
        second += jnp.sum(dnorm * normed, axis=-1, keepdims=True)
    first = first / width
    second = second / width

    def back(chunk):
        part = slice(chunk * cols, (chunk + 1) * cols)
        return inverse * (dn_ref[:, part] - first - normed_ref[:, part] * second)

    side = cols // 2
    for lo in range(2):
        for y in range(0, 4, 2):
            even, odd = back(2 * y + lo), back(2 * y + 2 + lo)
            for hi in range(2):
                cut = slice(hi * side, (hi + 1) * side)
                both = jnp.concatenate([even[:, cut], odd[:, cut]], axis=1)
                dproj_ref[hi * 2 + lo, :, (y // 2) * cols : (y // 2 + 1) * cols] = both.astype(jnp.bfloat16)
    for apart, ref in enumerate((first_ref, second_ref, third_ref, fourth_ref)):
        ref[...] = dproj_ref[lax.rem(x_ref[0] + 4 + x_ref[1] * apart, 4)]

def student(chip_x, own, received, residual, hot, table, head, guided):
    rows, width = residual.shape
    quarter = width // 4
    arrays = (own, *received, residual, hot, table, head, guided)
    outs = [(rows, quarter)] * 4 + [(rows, width), (rows, width), guided.shape]
    return pl.pallas_call(
        student_kernel,
        grid_spec=pltpu.PrefetchScalarGridSpec(
            num_scalar_prefetch=1,
            grid=(1,),
            in_specs=[
                pl.BlockSpec(array.shape, functools.partial(lambda dims, i, p: (0,) * dims, array.ndim))
                for array in arrays
            ],
            out_specs=[pl.BlockSpec(out, lambda i, p: (0, 0)) for out in outs],
            scratch_shapes=[
                pltpu.VMEM((rows, width), jnp.float32),
                pltpu.VMEM((rows, width), jnp.float32),
                pltpu.VMEM((rows, width), jnp.float32),
                pltpu.VMEM((4, rows, quarter), jnp.bfloat16),
            ],
        ),
        out_shape=[jax.ShapeDtypeStruct(out, jnp.bfloat16) for out in outs],
        compiler_params=pltpu.CompilerParams(vmem_limit_bytes=40 * 1024 * 1024),
        cost_estimate=FREE,
        name="student",
    )(chip_x, *arrays)


def sums_kernel(
    place_ref, in_ref, normed_ref, resid_ref, hot_ref, head_ref, own_ref, cross_ref, headpart_ref, mod_ref, out_ref
):
    f32, bf16 = jnp.float32, jnp.bfloat16
    chunks, cols, patch = headpart_ref.shape
    samples = mod_ref.shape[1]
    resid = resid_ref[...]
    hot = hot_ref[:, hot_ref.shape[1] - samples :]
    for i in range(chunks):
        part = slice(i * cols, (i + 1) * cols)
        cotangent = dot_f32(resid, head_ref[:, part], 1, 0)
        headpart_ref[i] = dot_f32(in_ref[:, part], resid, 0, 0)
        mod_ref[i] = dot_f32(hot, cotangent.astype(bf16), 0, 0)
        scaled = cotangent * normed_ref[:, part].astype(f32)
        mod_ref[chunks + i] = dot_f32(hot, scaled.astype(bf16), 0, 0)
    strip = cols // (2 * chunks)
    blank = jnp.zeros((strip, cols - chunks * patch), f32)
    for i in range(2 * chunks):
        take = slice(i * strip, (i + 1) * strip)
        head_rows = jnp.concatenate([headpart_ref[k, take, :] for k in range(chunks)] + [blank], axis=1)
        out_ref[i] = jnp.concatenate([head_rows, mod_ref[i]], axis=0).astype(bf16)
    for core, ref in enumerate((own_ref, cross_ref)):
        for pair in range(2):
            for chip in range(4):
                z, c, p = lax.rem(place_ref[0] + chip, 4), lax.rem(place_ref[1] + core, 2), lax.rem(place_ref[2] + pair, 2)
                ref[pair, chip] = out_ref[z * 4 + c * 2 + p]


def local_sums(place, model_in, normed, resid, hot, head, samples, devices):
    rows, width = model_in.shape
    chunk = 2 * width // devices
    part = (chunk // devices + samples, chunk)
    arrays = (model_in, normed, resid, hot, head)
    out = (2, devices // 4) + part
    return pl.pallas_call(
        sums_kernel,
        grid_spec=pltpu.PrefetchScalarGridSpec(
            num_scalar_prefetch=1,
            grid=(1,),
            in_specs=[pl.BlockSpec(array.shape, lambda i, p: (0, 0)) for array in arrays],
            out_specs=[pl.BlockSpec(out, lambda i, p: (0, 0, 0, 0)) for _ in range(2)],
            scratch_shapes=[
                pltpu.VMEM((devices // 2, chunk, head.shape[0]), jnp.float32),
                pltpu.VMEM((devices, samples, chunk), jnp.float32),
                pltpu.VMEM((devices,) + part, jnp.bfloat16),
            ],
        ),
        out_shape=[jax.ShapeDtypeStruct(out, jnp.bfloat16) for _ in range(2)],
        compiler_params=pltpu.CompilerParams(vmem_limit_bytes=24 * 1024 * 1024),
        cost_estimate=FREE,
        name="local_sums",
    )(place, *arrays)


def block_rows(refs, position):
    half = 64
    places = (position, position, 2 - position, 2 - position)
    return jnp.concatenate([ref[at * half : (at + 1) * half, :] for ref, at in zip(refs, places)], axis=0)


def early_kernel(*refs):
    out_ref, lefts, refs = refs[-1], refs[:4], refs[4:-1]
    total = jnp.zeros(out_ref.shape, jnp.float32)
    for arrival in range(4):
        rows = jnp.concatenate([refs[0][...], refs[1][...]], axis=0)
        total += dot_f32(lefts[0][arrival], rows, 1, 0)
        refs = refs[2:]
    for arrival in range(3):
        for position in range(3):
            total += dot_f32(lefts[1 + position][arrival], block_rows(refs[:4], position), 1, 0)
        refs = refs[4:]
    out_ref[...] = total


def early_product(lefts, mine, others):
    tile = 256
    flat = [part for blocks in (mine, others) for parts in blocks for part in parts]
    depth, width = lefts[0].shape[1], flat[0].shape[1]
    return pl.pallas_call(
        early_kernel,
        grid=(width // tile,),
        in_specs=[pl.BlockSpec(left.shape, lambda i: (0, 0, 0)) for left in lefts]
        + [pl.BlockSpec((part.shape[0], tile), lambda i: (0, i)) for part in flat],
        out_specs=pl.BlockSpec((depth, tile), lambda i: (0, i)),
        out_shape=jax.ShapeDtypeStruct((depth, width), jnp.float32),
        compiler_params=pltpu.CompilerParams(vmem_limit_bytes=50 * 1024 * 1024),
        cost_estimate=FREE,
        name="early_product",
    )(*lefts, *flat)


def late_kernel(y_ref, first_ref, second_ref, third_ref, a_ref, b_ref, c_ref, d_ref, early_ref, *refs):
    outs, turned_ref = refs[:-1], refs[-1]
    step = pl.program_id(0)
    tile = early_ref.shape[1]
    total = early_ref[...]
    for position, left in enumerate((first_ref, second_ref, third_ref)):
        total += dot_f32(left[0], block_rows((a_ref, b_ref, c_ref, d_ref), position), 1, 0)
    turned_ref[pl.ds(pl.multiple_of(step * tile, tile), tile), :] = total.T.astype(jnp.bfloat16)

    @pl.when(step == pl.num_programs(0) - 1)
    def _():
        rows = outs[0].shape[0]
        for apart, out in enumerate(outs):
            start = pl.multiple_of(lax.rem(y_ref[0] + apart, 4) * rows, rows)
            out[...] = turned_ref[pl.ds(start, rows), :]


def late_product(chip_y, lefts, flat, early):
    depth, width = early.shape
    tile = 256
    return pl.pallas_call(
        late_kernel,
        grid_spec=pltpu.PrefetchScalarGridSpec(
            num_scalar_prefetch=1,
            grid=(width // tile,),
            in_specs=[pl.BlockSpec((1,) + left.shape[1:], lambda i, p: (3, 0, 0)) for left in lefts]
            + [pl.BlockSpec((half.shape[0], tile), lambda i, p: (0, i)) for half in flat]
            + [pl.BlockSpec((depth, tile), lambda i, p: (0, i))],
            out_specs=[pl.BlockSpec((width // 4, depth), lambda i, p: (0, 0)) for _ in range(4)],
            scratch_shapes=[pltpu.VMEM((width, depth), jnp.bfloat16)],
        ),
        out_shape=[jax.ShapeDtypeStruct((width // 4, depth), jnp.bfloat16) for _ in range(4)],
        compiler_params=pltpu.CompilerParams(vmem_limit_bytes=VMEM_LIMIT),
        cost_estimate=FREE,
        name="late_product",
    )(chip_y, *lefts, *flat, early)


def local(
    teacher_hidden,
    student_query,
    student_key,
    student_value,
    residual,
    segment_ids,
    timesteps,
    guide_scales,
    time_proj,
    guide_proj,
    teach_head,
    stud_head,
    out_proj,
):
    bf16, f32 = jnp.bfloat16, jnp.float32
    seq_pos, pair_pos, data_pos = lax.axis_index("seq"), lax.axis_index("pair"), lax.axis_index("dp")
    chip_z, core = seq_pos // 2, seq_pos % 2
    chip_y, chip_x = data_pos // 2, pair_pos * 2 + data_pos % 2
    segment = segment_ids[0]
    samples = timesteps.shape[1]
    freq = time_proj.shape[0]

    guidance = guide_scales[0].astype(f32) / 8.0
    t_emb = sinusoid(timesteps[0].astype(f32), freq).astype(bf16)
    g_emb = sinusoid(1000.0 * guidance, freq).astype(bf16)
    teach_cols = jnp.dot(t_emb, time_proj, preferred_element_type=f32)
    stud_cols = teach_cols + jnp.dot(g_emb, guide_proj, preferred_element_type=f32)
    columns = jnp.concatenate([teach_cols, stud_cols], axis=0).astype(bf16)

    stud_rows = student_query.shape[1]
    ids = jnp.arange(2 * samples, dtype=jnp.int32)[None, :]
    hidden = teacher_hidden[0, 0]
    teach_seg = lax.dynamic_slice_in_dim(segment, seq_pos * hidden.shape[0], hidden.shape[0])
    stud_seg = lax.dynamic_slice_in_dim(teach_seg, pair_pos * stud_rows, stud_rows)
    teach_hot = (teach_seg[:, None] == ids).astype(bf16)
    stud_hot = (stud_seg[:, None] == ids - samples).astype(bf16)
    guide_tok = jnp.sum(
        jnp.where(stud_seg[:, None] == ids[:, :samples], guidance[None, :], 0.0), axis=1, keepdims=True
    )

    by_block = segment.reshape(8, 2, stud_rows)
    own_seg = lax.dynamic_index_in_dim(by_block, pair_pos, 1, keepdims=False)
    other_seg = lax.dynamic_index_in_dim(by_block, 1 - pair_pos, 1, keepdims=False)
    turn = jnp.arange(8, dtype=jnp.int32)
    away = ((1 - 2 * core) * (1 - 2 * (turn // 4)) * (turn % 4) + 4) % 4
    spots = (chip_z + away) % 4 * 2 + (core + turn // 4) % 2
    query_seg = own_seg[spots]
    low = jnp.sum((segment[None, :] < query_seg[:, :1]).astype(jnp.int32), axis=1) // 256
    high = (jnp.sum((segment[None, :] <= query_seg[:, -1:]).astype(jnp.int32), axis=1) + 255) // 256
    segs = query_seg[:, :, None], jnp.concatenate([own_seg, other_seg], axis=1)[:, None, :]

    key_crossed, weights_crossed = pair_swap(student_key[0]), core_swap(out_proj)
    first = exchange([student_value[0], student_query[0]], columns)
    first, key_crossed = lax.optimization_barrier((first, key_crossed))
    value_own, table = take_rows(first, (0, stud_rows), (2 * stud_rows, columns.shape[0]))
    value_own, table_other = lax.optimization_barrier((value_own, pair_swap(table)))
    value_other = pair_swap(value_own)
    second = exchange([student_key[0], key_crossed])
    lower, upper = jnp.where(pair_pos == 0, table, table_other), jnp.where(pair_pos == 0, table_other, table)
    table = jnp.stack([lower, upper], axis=1).reshape((16,) + columns.shape)
    velocity = teacher(hidden, teach_hot, table, teach_head.T)
    own_vel = lax.dynamic_slice_in_dim(velocity, pair_pos * stud_rows, stud_rows, 0)
    sent_vel = lax.dynamic_slice_in_dim(velocity, (1 - pair_pos) * stud_rows, stud_rows, 0)
    value_other, second, weights_crossed, low, high, segs, sent_vel = lax.optimization_barrier(
        (value_other, second, weights_crossed, low, high, segs, sent_vel)
    )
    attn_own, attn_cross, turned = attend(
        low, high, spots, *segs, value_other, first, second
    )

    own, *terms = project(attn_own, core_swap(attn_cross), out_proj, weights_crossed)
    received = ring_reduce(terms[4::-2], terms[5::-2])
    lefts = [turned]
    for _ in range(2):
        lefts.append(x_shift(lefts[-1], 1))
    other_vel = pair_swap(sent_vel.astype(bf16)).astype(f32)
    cond_vel = jnp.where(pair_pos == 0, own_vel, other_vel)
    uncond_vel = jnp.where(pair_pos == 0, other_vel, own_vel)
    guided = uncond_vel + guide_tok * (cond_vel - uncond_vel)
    own, lefts[1:3], guided = lax.optimization_barrier((own, lefts[1:3], guided))

    x_at = jnp.stack([chip_x, 1 - 2 * core]).astype(jnp.int32)
    y_at = jnp.reshape(chip_y, (1,)).astype(jnp.int32)
    *quarters, model_in, normed, resid = student(
        x_at, own, received, residual[0], stud_hot, table, stud_head.T, guided
    )

    from_x = [x_shift(quarters[apart], apart) for apart in (1, 2, 3)]
    mine = [quarters[0], seq_ring(quarters[0])]
    at = jnp.stack([chip_z, core, pair_pos]).astype(jnp.int32)
    kept, sent = local_sums(at, model_in, normed, resid, stud_hot, stud_head.T, samples, table.shape[0])
    from_x, kept, sent, mine[1] = lax.optimization_barrier((from_x, kept, sent, mine[1]))
    for _ in range(2):
        mine.append(seq_ring(mine[-1]))
    mine = [(block, core_swap(block)) for block in mine]
    came = core_swap(sent)
    kept, sent = add_rows(kept[0], came[0]), add_rows(kept[1], came[1])
    came = pair_swap(sent)
    came, lefts[2] = lax.optimization_barrier((came, lefts[2]))
    lefts.append(x_shift(lefts[2], 1))
    others = list(zip(*[ring_gather(half) for half in join(from_x)]))
    kept = add_rows(kept, came)
    sums = kept[0].astype(f32)
    for apart in (1, 2, 3):
        sums = sums + seq_shift(kept[apart], apart).astype(f32)
    sums = sums.astype(bf16)
    others_crossed = [tuple(core_swap(half) for half in pair) for pair in others[:3]]
    early = early_product(lefts, mine, [own + crossed for own, crossed in zip(others, others_crossed)])
    early, last = lax.optimization_barrier((early, others[3]))
    product = late_product(y_at, lefts[1:], [*last, *[core_swap(half) for half in last]], early)

    strip, patch, cols = sums.shape[0] - samples, stud_head.shape[1], sums.shape[1]
    head_sums = sums[:strip, : 8 * patch].reshape(strip, 8, patch).transpose(1, 0, 2)
    d_mod = jnp.broadcast_to(sums[None, strip:], (8, samples, cols))
    emb = g_emb.reshape(samples, 8, freq // 8).transpose(1, 0, 2)
    sent = jnp.concatenate(
        [
            jnp.pad(head_sums, ((0, 0), (0, 0), (0, 128 - patch))),
            jnp.pad(d_mod, ((0, 0), (0, strip - samples), (0, 0))),
            jnp.pad(emb, ((0, 0), (0, strip - samples), (0, 128 - freq // 8))),
        ],
        axis=2,
    )
    got = lax.all_to_all(sent, "dp", 0, 0, tiled=True)
    grad_head = jnp.sum(got[:, :, :patch].astype(f32), axis=0)
    d_mods = got[:, :samples, 128 : 128 + cols].reshape(8 * samples, cols)
    embs = got[:, :samples, 128 + cols : 128 + cols + freq // 8].reshape(8 * samples, freq // 8)
    grad_guidance = dot_f32(embs, d_mods, 0, 0)

    total = product[0].astype(f32)
    for apart in (2, 1, 3):
        total = total + y_shift(product[apart], apart).astype(f32)
    grad_out_proj = total.T
    return (grad_out_proj, grad_head, grad_guidance)


def solution(mesh):
    placed = (
        P("pair", "dp", "seq", None),
        P("dp", ("seq", "pair"), None),
        P("dp", ("seq", "pair"), None),
        P("dp", ("seq", "pair"), None),
        P("dp", ("seq", "pair"), None),
        P("dp", None),
        P("dp", None),
        P("dp", None),
        P(None, ("seq", "pair")),
        P(None, ("seq", "pair")),
        P(),
        P(),
        P("seq", None),
    )
    return jax.shard_map(
        local,
        mesh=mesh,
        in_specs=placed,
        out_specs=(
            P("seq", ("dp", "pair")),
            P(("dp", "seq", "pair"), None),
            P("dp", ("seq", "pair")),
        ),
        check_vma=False,
    )
```
